128 devices in a mesh: wide: 16 (over y, x), narrow: 8 (over z, core).
Axes of the slice: x: 4, y: 4, z: 4, core: 2. Of those that a mesh axis runs over, the one named last changes fastest.
Arguments:
- plume_field: bfloat16 [20, 512, 256, 256], P(None, 'wide', 'narrow'), may hold values from -6 to 6
- spectral_weight: float32 [16, 16, 16, 800], P('wide', 'narrow'), may hold values from -0.015625 to 0.015625
- linear_weight: bfloat16 [20, 20], replicated, may hold values from -1.25 to 1.25
- channel_bias: float32 [20], replicated, may hold values from -3 to 3
Outputs:
- layer_out: bfloat16 [20, 512, 256, 256], P(None, 'wide', 'narrow')
The draws below stay inside these ranges and needn't reach their ends.
All inputs are finite; a program needn't handle non-finite values.
Results may differ from the reference program's by a relative error of at most 0.0053.
Values may be sent and summed in bfloat16 or wider, within the bound.
A program may use at most 128 MiB of HBM per device.

```python
import math
import jax
import jax.numpy as jnp
from jax import lax

C = 20
NX = 256
MODES = 16
NY = 512
NZ = 256


def block_levels(stream_key, shape, cuts, smallest, top_value):
    def one(dim, shards_of):
        heights = jax.random.uniform(jax.random.fold_in(jax.random.fold_in(stream_key, 6), dim), (shards_of,), jnp.float32, smallest / len(cuts), top_value / len(cuts))
        return jnp.repeat(jnp.exp(heights), shape[dim] // shards_of).reshape((-1,) + (1,) * (len(shape) - dim - 1))

    gain = one(*cuts[0])
    for cut in cuts[1:]:
        gain = gain * one(*cut)
    return gain


def normal_values(own_key, dims, width, bound, shards=(), kind=jnp.bfloat16):
    loudness = block_levels(own_key, dims, shards, -0.22, 0.18) if shards else 1.0
    values = jax.random.normal(own_key, dims, jnp.float32) * width * loudness
    return jnp.minimum(jnp.maximum(values, -bound), bound).astype(kind)


def setup_inputs(seed: int = 0) -> dict:
    splits = jax.random.split(jax.random.key(seed), 5)
    return {
        "plume_field": normal_values(splits[0], (C, NY, NZ, NX), 1.0, 6.0, ((1, 16), (2, 8))),
        "spectral_weight": normal_values(splits[1], (MODES, MODES, MODES, 2 * C * C), (2 * C * MODES * MODES * MODES) ** -0.5, 0.015625, ((0, 16), (1, 8)), jnp.float32),
        "linear_weight": normal_values(splits[2], (C, C), C ** -0.5, 1.25),
        "channel_bias": normal_values(splits[3], (C,), 0.5, 3.0, (), jnp.float32),
    }


def mode_table(length, mode_count, offset, cell_count):
    places = offset + jnp.arange(cell_count, dtype=jnp.int32)
    orders = jnp.arange(mode_count, dtype=jnp.int32)
    signed_freq = jnp.where(orders < mode_count // 2, orders, orders - mode_count)
    phase_int = jnp.mod(places[:, None] * signed_freq[None, :], length)
    angles = phase_int.astype(jnp.float32) * (2.0 * math.pi / length)
    return (jnp.cos(angles), jnp.sin(angles))

def line_tables(length, mode_count):
    places = jnp.arange(length, dtype=jnp.int32)
    orders = jnp.arange(mode_count, dtype=jnp.int32)
    phase_int = jnp.mod(places[:, None] * orders[None, :], length)
    angles = phase_int.astype(jnp.float32) * (2.0 * math.pi / length)
    cos_tab = jnp.cos(angles)
    sin_tab = jnp.sin(angles)
    forward = jnp.concatenate([cos_tab, -sin_tab], axis=1).astype(jnp.bfloat16)
    doubled = jnp.where(orders == 0, 1.0, 2.0).astype(jnp.float32)
    inverse = jnp.concatenate([(cos_tab * doubled[None, :]).T, (-sin_tab * doubled[None, :]).T], axis=0).astype(jnp.bfloat16)
    return (forward, inverse)

def rotate(spectrum, cos_tab, sin_tab, form, turn_sign):
    precise = lax.Precision.HIGHEST
    real_part = spectrum[:, 0]
    imag_part = spectrum[:, 1]
    cos_re = jnp.einsum(form, real_part, cos_tab, precision=precise)
    cos_im = jnp.einsum(form, imag_part, cos_tab, precision=precise)
    sin_re = jnp.einsum(form, real_part, sin_tab, precision=precise)
    sin_im = jnp.einsum(form, imag_part, sin_tab, precision=precise)
    out_re = cos_re - turn_sign * sin_im
    out_im = cos_im + turn_sign * sin_re
    return jnp.stack([out_re, out_im], axis=1)

def line_forward(slab, forward, spec_scale):
    channels, y_rows, z_rows, x_len = slab.shape
    flattened = jnp.dot(slab.reshape(channels * y_rows * z_rows, x_len), forward, preferred_element_type=jnp.float32) * spec_scale
    mode_count = forward.shape[1] // 2
    return flattened.reshape(channels, y_rows, z_rows, 2, mode_count).transpose(4, 3, 0, 1, 2)

def line_back(spectrum, inverse):
    mode_count, pair_count, channels, y_rows, z_rows = spectrum.shape
    flattened = spectrum.astype(jnp.bfloat16).transpose(2, 3, 4, 1, 0).reshape(channels * y_rows * z_rows, pair_count * mode_count)
    result = jnp.dot(flattened, inverse, preferred_element_type=jnp.float32)
    return result.reshape(channels, y_rows, z_rows, inverse.shape[1])

def mix_modes(spectrum, spectral_weight):
    precise = lax.Precision.HIGHEST
    x_modes, pair_count, channels, y_modes, z_modes = spectrum.shape
    mix_table = spectral_weight.reshape(x_modes, y_modes, z_modes, 2, channels, channels)
    real_w = mix_table[:, :, :, 0]
    imag_w = mix_table[:, :, :, 1]
    real_part = spectrum[:, 0]
    imag_part = spectrum[:, 1]
    form = 'abkio,aibk->aobk'
    out_re = jnp.einsum(form, real_w, real_part, precision=precise) - jnp.einsum(form, imag_w, imag_part, precision=precise)
    out_im = jnp.einsum(form, real_w, imag_part, precision=precise) + jnp.einsum(form, imag_w, real_part, precision=precise)
    return jnp.stack([out_re, out_im], axis=1)

def finish_layer(slab, spectral, linear_weight, channel_bias):
    channels = slab.shape[0]
    linear = jnp.dot(linear_weight, slab.reshape(channels, -1), preferred_element_type=jnp.float32).reshape(slab.shape)
    summed = spectral + linear + channel_bias[:, None, None, None]
    return jax.nn.gelu(summed, approximate=False).astype(jnp.bfloat16)

def reference(plume_field, spectral_weight, linear_weight, channel_bias):
    channels, y_total, z_total, x_total = plume_field.shape
    mode_count = spectral_weight.shape[0]
    forward, inverse = line_tables(x_total, mode_count)
    spec_scale = 1.0 / math.sqrt(x_total * y_total * z_total)
    block_rows = 8 if y_total % 8 == 0 else y_total
    n_blocks = y_total // block_rows
    block_ids = jnp.arange(n_blocks, dtype=jnp.int32)

    def forward_block(block_index):
        slab = lax.dynamic_slice_in_dim(plume_field, block_index * block_rows, block_rows, 1)
        return line_forward(slab, forward, spec_scale)
    stacked = lax.map(forward_block, block_ids)
    spectrum = stacked.transpose(1, 2, 3, 0, 4, 5).reshape(mode_count, 2, channels, y_total, z_total)
    cos_y, sin_y = mode_table(y_total, mode_count, 0, y_total)
    cos_z, sin_z = mode_table(z_total, mode_count, 0, z_total)
    spectrum = rotate(spectrum, cos_y, sin_y, 'mcyz,yk->mckz', -1.0)
    spectrum = rotate(spectrum, cos_z, sin_z, 'mckz,zj->mckj', -1.0)
    spectrum = mix_modes(spectrum, spectral_weight)
    spectrum = rotate(spectrum, cos_z, sin_z, 'mckj,zj->mckz', 1.0)
    spectrum = rotate(spectrum, cos_y, sin_y, 'mckz,yk->mcyz', 1.0).astype(jnp.bfloat16)

    def back_block(block_index):
        pieces = lax.dynamic_slice_in_dim(spectrum, block_index * block_rows, block_rows, 3)
        slab = lax.dynamic_slice_in_dim(plume_field, block_index * block_rows, block_rows, 1)
        return finish_layer(slab, line_back(pieces, inverse), linear_weight, channel_bias)
    outputs = lax.map(back_block, block_ids)
    return outputs.transpose(1, 0, 2, 3, 4).reshape(channels, y_total, z_total, x_total)
```

```python
import functools
import math

import jax
import jax.numpy as jnp
import ml_dtypes
import numpy as np
from jax import lax
from jax.experimental import pallas as pl
from jax.experimental.pallas import tpu as pltpu
from jax.sharding import PartitionSpec as P

MESH = pl.DeviceIdType.MESH
C, NX, NY, NZ, K = 20, 256, 512, 256, 16
YL, ZL = 32, 32
CELLS = YL * ZL
LANES = 2 * K * C
BF16, F32 = jnp.bfloat16, jnp.float32
GROUPS = ((0, 8, 0), (8, 8, 256), (16, 4, 512))
VMEM_LIMIT = 56 * 2**20


def np_bf16(a):
    return np.asarray(a, np.float32).astype(ml_dtypes.bfloat16)


def signed(m):
    return np.where(m < K // 2, m, m - K)


def x_tables():
    places, orders = np.arange(NX), np.arange(K)
    angles = np.mod(places[:, None] * orders[None, :], NX).astype(np.float32) * np.float32(2.0 * math.pi / NX)
    cos_tab, sin_tab = np.cos(angles), np.sin(angles)
    doubled = np.where(orders == 0, 1.0, 2.0).astype(np.float32)
    forward = np_bf16(np.stack([cos_tab, -sin_tab], -1))
    inverse = np_bf16(np.stack([cos_tab * doubled, -sin_tab * doubled], -1))
    return forward, inverse


def forward_table():
    forward = x_tables()[0].reshape(NX, 2 * K)
    wide = np.zeros((8, NX, 2 * K, 8), ml_dtypes.bfloat16)
    slim = np.zeros((4, NX, 2 * K, 4), ml_dtypes.bfloat16)
    for c in range(8):
        wide[c, :, :, c] = forward
    for c in range(4):
        slim[c, :, :, c] = forward
    return wide.reshape(8 * NX, 256), slim.reshape(4 * NX, 128)


def inverse_table():
    inverse = x_tables()[1].reshape(NX, 2 * K).T
    return np.repeat(inverse, 4, axis=0)


def cell_angles():
    f = signed(np.arange(K))
    y = np.mod(f[:, None] * np.arange(YL)[None, :], NY) / NY
    z = np.mod(f[:, None] * np.arange(ZL)[None, :], NZ) / NZ
    turns = y[:, None, :, None] + z[None, :, None, :]
    return 2.0 * math.pi * turns.reshape(K * K, CELLS)


def analysis_table():
    angles = cell_angles()
    return np_bf16(np.concatenate([np.cos(angles), np.sin(angles)], 0))


def synthesis_table():
    angles = cell_angles().T
    return np_bf16(np.concatenate([np.cos(angles), np.sin(angles)], 1))


def offset_phase(wide, narrow, rows):
    row = lax.broadcasted_iota(jnp.int32, (rows, 128), 0)
    j, l = row // K, row % K
    fj = jnp.where(j < K // 2, j, j - K)
    fl = jnp.where(l < K // 2, l, l - K)
    step = (fj * wide + 2 * fl * narrow) & 15
    cos_v = jnp.zeros((rows, 128), F32)
    sin_v = jnp.zeros((rows, 128), F32)
    for k in range(16):
        c, s = math.cos(math.pi * k / 8), math.sin(math.pi * k / 8)
        cos_v = jnp.where(step == k, F32(c), cos_v)
        sin_v = jnp.where(step == k, F32(s), sin_v)
    return cos_v, sin_v


def swap_pair(v, half):
    lanes = v.shape[1]
    lane = lax.broadcasted_iota(jnp.int32, v.shape, 1)
    return jnp.where((lane // half) % 2 == 0, pltpu.roll(v, lanes - half, 1), pltpu.roll(v, half, 1))


def lane_sign(shape, half):
    lane = lax.broadcasted_iota(jnp.int32, shape, 1)
    return jnp.where((lane // half) % 2 == 0, F32(1.0), F32(-1.0))


def row_of(pair, c):
    if c < 8:
        return pair * 8 + c
    if c < 16:
        return 16 + pair * 8 + c - 8
    return 32 + pair * 4 + c - 16


def spectra_kernel(
    n_wide, n_narrow,
    plume, w_ref, ta_ref, tb_ref, e_ref, m_ref,
    x_buf, a_buf, s_send, s_recv, t_send, t_recv, q_buf, wt_buf, m_send, m_recv, g_send, g_recv, phase,
    in_sem, s_ss, s_rs, t_ss, t_rs, m_ss, m_rs, g_ss, g_rs,
):
    wide, narrow = lax.axis_index("wide"), lax.axis_index("narrow")
    loads = []
    for g, (c0, nc, _) in enumerate(GROUPS):
        copy = pltpu.make_async_copy(plume.at[pl.ds(c0, nc)], x_buf.at[pl.ds(c0, nc)], in_sem.at[g])
        copy.start()
        loads.append(copy)

    barrier = pltpu.get_barrier_semaphore()

    def greet_narrow(i, _):
        pl.semaphore_signal(barrier, inc=1, device_id=(wide, lax.rem(narrow + i, n_narrow)), device_id_type=MESH)
        return 0

    def greet_wide(i, _):
        pl.semaphore_signal(barrier, inc=1, device_id=(lax.rem(wide + i, n_wide), narrow), device_id_type=MESH)
        return 0

    lax.fori_loop(1, n_narrow, greet_narrow, 0)
    lax.fori_loop(1, n_wide, greet_wide, 0)

    cos_v, sin_v = offset_phase(wide, narrow, K * K)
    phase[0] = cos_v
    phase[1] = sin_v
    for k in range(7):
        width = min(128, 2 * C * C - 128 * k)
        wt_buf[pl.ds(128 * k, width), :] = w_ref[:, pl.ds(128 * k, width)].T
    scale = F32(1.0 / math.sqrt(NX * NY * NZ))

    def s_copy(g, i):
        _, nc, lane0 = GROUPS[g]
        to = lax.rem(narrow + i, n_narrow)
        lanes = pl.ds(lane0, 32 * nc)
        return pltpu.make_async_remote_copy(
            src_ref=s_send.at[to, :, lanes], dst_ref=s_recv.at[i, :, lanes],
            send_sem=s_ss.at[g, i], recv_sem=s_rs.at[g, i],
            device_id=(wide, to), device_id_type=MESH)

    for g, (c0, nc, lane0) in enumerate(GROUPS):
        loads[g].wait()
        table = ta_ref if nc == 8 else tb_ref
        width = 32 * nc
        for r in range(4):
            rows = jnp.concatenate(
                [x_buf[c, pl.ds(8 * r, 8)].reshape(256, NX) for c in range(c0, c0 + nc)], axis=1)
            a_buf[pl.ds(256 * r, 256), pl.ds(0, width)] = jnp.dot(
                rows, table[...], preferred_element_type=F32).astype(BF16)
        a = a_buf[:, pl.ds(0, width)]
        half = nc
        for h in range(2):
            rows = pl.ds(128 * h, 128)
            g_cos = jnp.dot(e_ref[rows, :], a, preferred_element_type=F32)
            g_sin = jnp.dot(e_ref[pl.ds(256 + 128 * h, 128), :], a, preferred_element_type=F32)
            for part in range(width // 128):
                lanes = slice(128 * part, 128 * part + 128)
                gc, gs = g_cos[:, lanes], g_sin[:, lanes]
                pc, ps = phase[0, rows] * scale, phase[1, rows] * scale
                rc = pc * gc - ps * gs
                rs = ps * gc + pc * gs
                s = rc + lane_sign((128, 128), half) * swap_pair(rs, half)
                s_send[pl.ds(4 * h, 4), :, pl.ds(lane0 + 128 * part, 128)] = s.astype(BF16).reshape(4, 32, 128)
        if g == 0:
            pl.semaphore_wait(barrier, n_narrow + n_wide - 2)

        def send(i, _, g=g):
            s_copy(g, i).start()
            return 0

        lax.fori_loop(1, n_narrow, send, 0)

    s_recv[0] = s_send[narrow]
    for g in range(len(GROUPS)):
        def arrive(i, _, g=g):
            s_copy(g, i).wait_recv()
            return 0

        lax.fori_loop(1, n_narrow, arrive, 0)
    total = s_recv[0].astype(F32)
    for i in range(1, n_narrow):
        total = total + s_recv[i].astype(F32)

    for k in range(K):
        pieces = [total[:, 16 * k:16 * k + 16], total[:, 256 + 16 * k:256 + 16 * k + 16],
                  total[:, 512 + 8 * k:512 + 8 * k + 8]]
        row = jnp.concatenate(pieces, axis=1)
        pad = jnp.zeros((16, 24), F32)
        t_send[k] = jnp.concatenate([row[:16], pad, row[16:], pad], axis=1).astype(BF16)

    def t_copy(i):
        to = lax.rem(wide + i, n_wide)
        return pltpu.make_async_remote_copy(
            src_ref=t_send.at[to], dst_ref=t_recv.at[i], send_sem=t_ss.at[i], recv_sem=t_rs.at[i],
            device_id=(to, narrow), device_id_type=MESH)

    def t_start(i, _):
        t_copy(i).start()
        return 0

    def t_arrive(i, _):
        t_copy(i).wait_recv()
        return 0

    lax.fori_loop(1, n_wide, t_start, 0)
    t_recv[0] = t_send[wide]
    lax.fori_loop(1, n_wide, t_arrive, 0)
    total = t_recv[0].astype(F32)
    for i in range(1, n_wide):
        total = total + t_recv[i].astype(F32)
    turned = total.T
    q_buf[...] = jnp.concatenate([turned[0:64], turned[64:128]], axis=1)

    out_re = jnp.zeros((C, 32), F32)
    out_im = jnp.zeros((C, 32), F32)
    for c in range(C):
        s_re = q_buf[pl.ds(row_of(0, c), 1), :]
        s_im = q_buf[pl.ds(row_of(1, c), 1), :]
        w_re = wt_buf[pl.ds(C * c, C), :]
        w_im = wt_buf[pl.ds(C * C + C * c, C), :]
        out_re = out_re + (w_re * s_re - w_im * s_im)
        out_im = out_im + (w_re * s_im + w_im * s_re)
    rows = []
    for j in range(5):
        rows += [out_re[4 * j:4 * j + 4], out_im[4 * j:4 * j + 4]]
    rows.append(jnp.zeros((24, 32), F32))
    rows = jnp.concatenate(rows, axis=0)
    rows = jnp.concatenate([rows[:, :16], rows[:, 16:]], axis=0)
    m_send[...] = rows.T.astype(BF16)

    def m_copy(i):
        to = lax.rem(wide + i, n_wide)
        return pltpu.make_async_remote_copy(
            src_ref=m_send, dst_ref=m_recv.at[wide], send_sem=m_ss.at[i], recv_sem=m_rs.at[i],
            device_id=(to, narrow), device_id_type=MESH)

    def m_start(i, _):
        m_copy(i).start()
        return 0

    def m_arrive(i, _):
        m_copy(i).wait_recv()
        return 0

    lax.fori_loop(1, n_wide, m_start, 0)
    m_recv[wide] = m_send[...]
    lax.fori_loop(1, n_wide, m_arrive, 0)
    tiles = [m_recv[k].astype(F32) for k in range(K)]
    for j2 in range(2):
        for j in range(5):
            at = 64 * j2 + 8 * j
            lanes = jnp.concatenate([tiles[k][:, at:at + 8] for k in range(K)], axis=1)
            g_send[pl.ds(16 * j2, 16), pl.ds(128 * j, 128)] = lanes.astype(BF16)

    def g_copy(i):
        to = lax.rem(narrow + i, n_narrow)
        return pltpu.make_async_remote_copy(
            src_ref=g_send, dst_ref=g_recv.at[narrow], send_sem=g_ss.at[i], recv_sem=g_rs.at[i],
            device_id=(wide, to), device_id_type=MESH)

    def g_start(i, _):
        g_copy(i).start()
        return 0

    def g_arrive(i, _):
        g_copy(i).wait_recv()
        return 0

    lax.fori_loop(1, n_narrow, g_start, 0)
    g_recv[narrow] = g_send[...]
    lax.fori_loop(1, n_narrow, g_arrive, 0)

    for j in range(n_narrow):
        pc, ps = phase[0, pl.ds(32 * j, 32)], phase[1, pl.ds(32 * j, 32)]
        for part in range(5):
            v = g_recv[j, :, pl.ds(128 * part, 128)].astype(F32)
            sw = -lane_sign((32, 128), 4) * swap_pair(v, 4)
            m_ref[pl.ds(32 * j, 32), pl.ds(128 * part, 128)] = (pc * v + ps * sw).astype(BF16)
            m_ref[pl.ds(256 + 32 * j, 32), pl.ds(128 * part, 128)] = (pc * sw - ps * v).astype(BF16)

    def drain_narrow(i, _):
        for g in range(len(GROUPS)):
            s_copy(g, i).wait_send()
        g_copy(i).wait_send()
        return 0

    def drain_wide(i, _):
        t_copy(i).wait_send()
        m_copy(i).wait_send()
        return 0

    lax.fori_loop(1, n_narrow, drain_narrow, 0)
    lax.fori_loop(1, n_wide, drain_wide, 0)


def spectra(n_wide, n_narrow, plume, weight, ta, tb, e):
    vmem = pl.BlockSpec(memory_space=pltpu.VMEM)
    dma = pltpu.SemaphoreType.DMA
    return pl.pallas_call(
        functools.partial(spectra_kernel, n_wide, n_narrow),
        out_shape=jax.ShapeDtypeStruct((2 * K * K, LANES), BF16),
        in_specs=[pl.BlockSpec(memory_space=pl.ANY)] + [vmem] * 4,
        out_specs=vmem,
        scratch_shapes=[
            pltpu.VMEM((C, YL, ZL, NX), BF16),
            pltpu.VMEM((CELLS, 256), BF16),
            pltpu.VMEM((n_narrow, 32, LANES), BF16),
            pltpu.VMEM((n_narrow, 32, LANES), BF16),
            pltpu.VMEM((K, 16, 128), BF16),
            pltpu.VMEM((n_wide, 16, 128), BF16),
            pltpu.VMEM((64, 32), F32),
            pltpu.VMEM((2 * C * C, 32), F32),
            pltpu.VMEM((16, 128), BF16),
            pltpu.VMEM((n_wide, 16, 128), BF16),
            pltpu.VMEM((32, LANES), BF16),
            pltpu.VMEM((n_narrow, 32, LANES), BF16),
            pltpu.VMEM((2, K * K, 128), F32),
            dma((3,)),
            dma((3, n_narrow)), dma((3, n_narrow)),
            dma((n_wide,)), dma((n_wide,)),
            dma((n_wide,)), dma((n_wide,)),
            dma((n_narrow,)), dma((n_narrow,)),
        ],
        compiler_params=pltpu.CompilerParams(
            collective_id=0, has_side_effects=True, vmem_limit_bytes=VMEM_LIMIT),
        name="spectra",
    )(plume, weight, ta, tb, e)


CHUNKS = 4


def output_kernel(plume, m_ref, e_ref, lw_ref, bias_ref, xi_ref, out, x_buf, o_buf, b_buf, kron, rhs, in_sem, out_sem):
    yt = YL // CHUNKS

    def load(i):
        rows = pl.ds(i * yt, yt)
        return pltpu.make_async_copy(plume.at[:, rows], x_buf.at[:, rows], in_sem.at[i])

    def store(i):
        rows = pl.ds(i * yt, yt)
        return pltpu.make_async_copy(o_buf.at[:, rows], out.at[:, rows], out_sem.at[i])

    for i in range(CHUNKS):
        load(i).start()
    spread = jnp.where(
        lax.broadcasted_iota(jnp.int32, (320, C), 0) // 16 == lax.broadcasted_iota(jnp.int32, (320, C), 1),
        F32(1.0), F32(0.0)).astype(BF16)
    rows20 = jnp.dot(spread, lw_ref[...], preferred_element_type=F32).astype(BF16)
    across = jnp.where(
        lax.broadcasted_iota(jnp.int32, (C, 384), 1) // 16 == lax.broadcasted_iota(jnp.int32, (C, 384), 0),
        F32(1.0), F32(0.0)).astype(BF16)
    full = jnp.dot(rows20, across, preferred_element_type=F32)
    row = lax.broadcasted_iota(jnp.int32, (320, 384), 0)
    col = lax.broadcasted_iota(jnp.int32, (320, 384), 1)
    full = jnp.where((row % 16) == (col % 16), full, F32(0.0))
    bias = bias_ref[...]
    b1 = bias.astype(BF16).astype(F32)
    b2 = (bias - b1).astype(BF16).astype(F32)
    b3 = bias - b1 - b2
    full = jnp.where(col == 320, b1, full)
    full = jnp.where(col == 321, b2, full)
    full = jnp.where(col == 322, b3, full)
    kron[...] = full.astype(BF16)
    for s in range(2):
        rhs[s, pl.ds(0, 128), :] = xi_ref[...]
        rhs[s, pl.ds(192, 64), :] = jnp.where(
            lax.broadcasted_iota(jnp.int32, (64, NX), 0) < 16, F32(1.0), F32(0.0)).astype(BF16)
    lane = lax.broadcasted_iota(jnp.int32, (16, 128), 1) % 4
    masks = [lane == k for k in range(4)]

    def chunk(i, _):
        load(i).wait()
        cells = yt * ZL
        b_buf[...] = jnp.dot(
            e_ref[pl.ds(pl.multiple_of(i * cells, cells), cells), :], m_ref[...],
            preferred_element_type=F32).astype(BF16)
        for q in range(cells // 16):
            y, z, s = i * yt + q // 2, (q % 2) * 16, q % 2
            xs = x_buf[:, y, pl.ds(z, 16), :].reshape(320, NX)
            rhs[s, pl.ds(128, 64), :] = xs[256:]
            parts = []
            for o in range(C):
                v = b_buf[pl.ds(16 * q, 16), pl.ds(128 * (o // 4), 128)]
                parts.append(jnp.where(masks[o % 4], v, jnp.zeros_like(v)))
            left = jnp.concatenate([jnp.concatenate(parts, 0), kron[:, pl.ds(256, 128)]], 1)
            acc = jnp.dot(kron[:, pl.ds(0, 256)], xs[:256], preferred_element_type=F32)
            acc = acc + jnp.dot(left, rhs[s], preferred_element_type=F32)
            half = 0.5 * acc
            y_out = half + half * lax.erf(acc * F32(math.sqrt(0.5)))
            o_buf[:, y, pl.ds(z, 16), :] = y_out.astype(BF16).reshape(C, 16, NX)
        store(i).start()
        return 0

    lax.fori_loop(0, CHUNKS, chunk, 0)
    for i in range(CHUNKS):
        store(i).wait()


def output(plume, m, e, lw, bias, xi):
    vmem = pl.BlockSpec(memory_space=pltpu.VMEM)
    anywhere = pl.BlockSpec(memory_space=pl.ANY)
    dma = pltpu.SemaphoreType.DMA
    return pl.pallas_call(
        output_kernel,
        out_shape=jax.ShapeDtypeStruct((C, YL, ZL, NX), BF16),
        in_specs=[anywhere] + [vmem] * 5,
        out_specs=anywhere,
        scratch_shapes=[
            pltpu.VMEM((C, YL, ZL, NX), BF16),
            pltpu.VMEM((C, YL, ZL, NX), BF16),
            pltpu.VMEM((CELLS // CHUNKS, LANES), BF16),
            pltpu.VMEM((320, 384), BF16),
            pltpu.VMEM((2, 256, NX), BF16),
            dma((CHUNKS,)), dma((CHUNKS,)),
        ],
        compiler_params=pltpu.CompilerParams(vmem_limit_bytes=VMEM_LIMIT),
        name="output",
    )(plume, m, e, lw, bias, xi)


def on_device(n_wide, n_narrow, plume, weight, linear_weight, channel_bias):
    ta, tb = forward_table()
    m = spectra(
        n_wide, n_narrow, plume, weight.reshape(32, 2 * C * C),
        jnp.asarray(ta), jnp.asarray(tb), jnp.asarray(analysis_table()))
    bias = jnp.repeat(channel_bias, 16)[:, None]
    return output(
        plume, m, jnp.asarray(synthesis_table()), linear_weight, bias, jnp.asarray(inverse_table()))


def solution(mesh):
    n_wide, n_narrow = mesh.shape["wide"], mesh.shape["narrow"]
    return jax.shard_map(
        functools.partial(on_device, n_wide, n_narrow), mesh=mesh,
        in_specs=(P(None, "wide", "narrow", None), P("wide", "narrow", None, None), P(), P()),
        out_specs=P(None, "wide", "narrow", None), check_vma=False)
```

```python
import math

import jax
import jax.numpy as jnp
import ml_dtypes
import numpy as np
from jax import lax
from jax.experimental import pallas as pl
from jax.experimental.pallas import tpu as pltpu
from jax.sharding import PartitionSpec as P

MESH = pl.DeviceIdType.MESH
C, NX, NY, NZ, K = 20, 256, 512, 256, 16
YL, ZL = 32, 32
CELLS = YL * ZL
LANES = 2 * K * C
BF16, F32 = jnp.bfloat16, jnp.float32
GROUPS = ((0, 8, 0), (8, 8, 256), (16, 4, 512))
CONTRACT_LANES = (((1,), (1,)), ((), ()))


def np_bf16(a):
    return np.asarray(a, np.float32).astype(ml_dtypes.bfloat16)


def signed(m):
    return np.where(m < K // 2, m, m - K)


def x_tables():
    places, orders = np.arange(NX), np.arange(K)
    angles = np.mod(places[:, None] * orders[None, :], NX).astype(np.float32) * np.float32(2.0 * math.pi / NX)
    cos_tab, sin_tab = np.cos(angles), np.sin(angles)
    doubled = np.where(orders == 0, 1.0, 2.0).astype(np.float32)
    forward = np_bf16(np.stack([cos_tab, -sin_tab], -1))
    inverse = np_bf16(np.stack([cos_tab * doubled, -sin_tab * doubled], -1))
    return forward, inverse


def forward_table():
    forward = x_tables()[0].reshape(NX, 2 * K).T
    return np.repeat(forward, 8, axis=0), np.repeat(forward, 4, axis=0)


def inverse_table():
    inverse = x_tables()[1].reshape(NX, 2 * K).T
    return np.repeat(inverse, 4, axis=0)


def mode_order():
    core, z, j2, l = np.meshgrid(np.arange(2), np.arange(4), np.arange(2), np.arange(K), indexing="ij")
    return (2 * (2 * z + core) + j2).reshape(-1), l.reshape(-1)


def cell_angles():
    j, l = mode_order()
    fj, fl = signed(j), signed(l)
    y = np.mod(fj[:, None] * np.arange(YL)[None, :], NY) / NY
    z = np.mod(fl[:, None] * np.arange(ZL)[None, :], NZ) / NZ
    turns = y[:, :, None] + z[:, None, :]
    return 2.0 * math.pi * turns.reshape(K * K, CELLS)


def mode_table():
    angles = cell_angles().T
    return np_bf16(np.concatenate([np.cos(angles), np.sin(angles)], 1))


def offset_phase(wide, narrow):
    lane = lax.broadcasted_iota(jnp.int32, (8, 256), 1)
    l = lane % 16
    j = 2 * (2 * ((lane // 32) % 4) + lane // 128) + (lane // 16) % 2
    fj = jnp.where(j < K // 2, j, j - K)
    fl = jnp.where(l < K // 2, l, l - K)
    step = (fj * wide + 2 * fl * narrow) & 15
    cos_v = jnp.zeros((8, 256), F32)
    sin_v = jnp.zeros((8, 256), F32)
    for k in range(16):
        c, s = math.cos(math.pi * k / 8), math.sin(math.pi * k / 8)
        cos_v = jnp.where(step == k, F32(c), cos_v)
        sin_v = jnp.where(step == k, F32(s), sin_v)
    return cos_v, sin_v


def row_of(pair, c):
    if c < 8:
        return pair * 8 + c
    if c < 16:
        return 16 + pair * 8 + c - 8
    return 32 + pair * 4 + c - 16


def block_turn(tiles):
    shape = tiles[0].shape
    block = lax.broadcasted_iota(jnp.int32, shape, len(shape) - 1) // 32
    out = []
    for r in range(4):
        v = tiles[r]
        for b in range(4):
            if b != r:
                v = jnp.where(block == b, pltpu.roll(tiles[b], (32 * (b - r)) % 128, len(shape) - 1), v)
        out.append(v)
    return out


def spectra_kernel(
    plume, w_hbm, t8_hbm, t4_hbm, e_ref,
    m_ref,
    x_buf, w_ref, t8_ref, t4_ref, e_buf, tab8, tab4, a_buf, sib_send, sib_recv, mine, s_send, s_recv, q_buf, wt_buf, m_send, m_recv,
    g_buf, phase,
    in_sem, w_sem, e_sem, c_ss, c_rs, s_ss, s_rs, m_ss, m_rs, g_ss, g_rs,
):
    wide, narrow = lax.axis_index("wide"), lax.axis_index("narrow")
    y, x = lax.div(wide, 4), lax.rem(wide, 4)
    z, core = lax.div(narrow, 2), lax.rem(narrow, 2)
    sibling = (wide, narrow + 1 - 2 * core)
    e_copy = pltpu.make_async_copy(e_ref, e_buf, e_sem)
    small = [pltpu.make_async_copy(src, dst, w_sem.at[i]) for i, (src, dst) in enumerate(
        ((t8_hbm, t8_ref), (t4_hbm, t4_ref), (w_hbm, w_ref)))]
    for copy in small:
        copy.start()
    loads = []
    for g, (c0, nc, _) in enumerate(GROUPS):
        copy = pltpu.make_async_copy(plume.at[pl.ds(c0, nc)], x_buf.at[pl.ds(c0, nc)], in_sem.at[g])
        copy.start()
        loads.append(copy)
        if g == 0:
            e_copy.start()

    rows_of_chips = [4 * lax.rem(y + d, 4) for d in range(4)]
    places = [lax.rem(x + d, 4) for d in range(4)]
    wides = [[r + p for p in places] for r in rows_of_chips]
    layers = [lax.rem(z + d, 4) for d in range(4)]
    narrows = [2 * v + core for v in layers]
    far = (0, 1, 2, 1)
    others = sorted(
        [(16 * dz + 4 * dy + dx, dz, dy, dx) for dz in range(4) for dy in range(4) for dx in range(4)][1:],
        key=lambda v: (-(far[v[1]] + far[v[2]] + far[v[3]]), v))

    barrier = pltpu.get_barrier_semaphore()
    pl.semaphore_signal(barrier, inc=1, device_id=sibling, device_id_type=MESH)

    for _, dz, dy, dx in others:
        pl.semaphore_signal(barrier, inc=1, device_id=(wides[dy][dx], narrows[dz]), device_id_type=MESH)

    for copy in small:
        copy.wait()
    r8 = lax.broadcasted_iota(jnp.int32, (256, NX), 0) % 8
    r4 = lax.broadcasted_iota(jnp.int32, (128, NX), 0) % 4
    for c in range(8):
        tab8[:, pl.ds(NX * c, NX)] = jnp.where(r8 == c, t8_ref[...], jnp.zeros((), BF16))
    for c in range(4):
        tab4[:, pl.ds(NX * c, NX)] = jnp.where(r4 == c, t4_ref[...], jnp.zeros((), BF16))
    cos_v, sin_v = offset_phase(wide, narrow)
    for h in range(2):
        phase[0, h] = cos_v[:, 128 * h:128 * h + 128]
        phase[1, h] = sin_v[:, 128 * h:128 * h + 128]
    scale = F32(1.0 / math.sqrt(NX * NY * NZ))
    pc, ps = cos_v * scale, sin_v * scale
    for k in range(7):
        width = min(128, 2 * C * C - 128 * k)
        wt_buf[pl.ds(128 * k, width), :] = w_ref[:, pl.ds(128 * k, width)].T

    def c_copy(g):
        c0, nc, row0 = GROUPS[g]
        rows = pl.ds(row0, 32 * nc)
        return pltpu.make_async_remote_copy(
            src_ref=sib_send.at[1 - core, rows], dst_ref=sib_recv.at[rows],
            send_sem=c_ss.at[g], recv_sem=c_rs.at[g], device_id=sibling, device_id_type=MESH)

    for g, (c0, nc, row0) in enumerate(GROUPS):
        loads[g].wait()
        table = tab8 if nc == 8 else tab4
        width = 32 * nc
        for r in range(4):
            rows = jnp.concatenate(
                [x_buf[c, pl.ds(8 * r, 8)].reshape(256, NX) for c in range(c0, c0 + nc)], axis=1)
            a_buf[pl.ds(0, width), pl.ds(256 * r, 256)] = lax.dot_general(
                table[...], rows, CONTRACT_LANES, preferred_element_type=F32).astype(BF16)
        if g == 0:
            e_copy.wait()
        turned = jnp.dot(a_buf[pl.ds(0, width), :], e_buf[...], preferred_element_type=F32)
        g_cos = turned[:, :256].reshape(width // 8, 8, 256)
        g_sin = turned[:, 256:].reshape(width // 8, 8, 256)
        rc = pc * g_cos - ps * g_sin
        rs = ps * g_cos + pc * g_sin
        if nc == 8:
            rc, rs = rc.reshape(K, 2, 8, 256), rs.reshape(K, 2, 8, 256)
            s = jnp.stack([rc[:, 0] + rs[:, 1], rc[:, 1] - rs[:, 0]], axis=1)
        else:
            first = lax.broadcasted_iota(jnp.int32, (K, 8, 256), 1) < 4
            turn = pltpu.roll(rs, 4, 1)
            s = rc + jnp.where(first, turn, -turn)
        s = s.reshape(width, 256)
        sib_send[0, pl.ds(row0, width), :] = s[:, :128].astype(BF16)
        sib_send[1, pl.ds(row0, width), :] = s[:, 128:].astype(BF16)
        mine[pl.ds(row0, width), :] = jnp.where(core == 0, s[:, :128], s[:, 128:])
        if g == 0:
            pl.semaphore_wait(barrier, 64)
        c_copy(g).start()

    for g in range(len(GROUPS)):
        c_copy(g).wait_recv()

    def both(g, size):
        _, nc, row0 = GROUPS[g]
        rows = pl.ds(row0, 32 * nc)
        return (mine[rows, :] + sib_recv[rows, :].astype(F32)).reshape(size)

    g0, g1, g2 = both(0, (K, 2, 8, 128)), both(1, (K, 2, 8, 128)), both(2, (K, 8, 128))
    dense = block_turn([g0[:, 0], g0[:, 1], g1[:, 0], g1[:, 1]])
    for r in range(4):
        rest = g2 if r == 0 else pltpu.roll(g2, 128 - 32 * r, 2)
        s_send[r] = jnp.concatenate([dense[r], rest], axis=1).astype(BF16)

    for slot, dz, dy, dx in others:
        pltpu.make_async_remote_copy(
            src_ref=s_send.at[layers[dz], wides[dy][dx]], dst_ref=s_recv.at[slot],
            send_sem=s_ss, recv_sem=s_rs.at[dz],
            device_id=(wides[dy][dx], narrows[dz]), device_id_type=MESH).start()

    def arrived(buf, sems, part):
        ref = buf.at[pl.ds(max(1, 16 * part), 16 if part else 15)]
        pltpu.make_async_copy(ref, ref, sems.at[part]).wait()

    total = s_send[z, wide].astype(F32)
    for part in (0, 1, 3, 2):
        first = max(1, 16 * part)
        arrived(s_recv, s_rs, part)
        total = total + jnp.sum(s_recv[pl.ds(first, 16 * part + 16 - first)].astype(F32), axis=0)
    for t in range(4):
        v = total[0:8] if t == 0 else pltpu.roll(total[0:8], 128 - 32 * t, 1)
        q_buf[pl.ds(8 * t, 8), :] = v[:, :32]
    q_buf[pl.ds(32, 8), :] = total[8:16, :32]

    out_re = jnp.zeros((C, 32), F32)
    out_im = jnp.zeros((C, 32), F32)
    for c in range(C):
        s_re = q_buf[pl.ds(row_of(0, c), 1), :]
        s_im = q_buf[pl.ds(row_of(1, c), 1), :]
        w_re = wt_buf[pl.ds(C * c, C), :]
        w_im = wt_buf[pl.ds(C * C + C * c, C), :]
        out_re = out_re + (w_re * s_re - w_im * s_im)
        out_im = out_im + (w_re * s_im + w_im * s_re)
    tiles = [jnp.concatenate([out_re[4 * j:4 * j + 4], out_im[4 * j:4 * j + 4]], axis=0) for j in range(5)]
    m_send[...] = jnp.concatenate(
        [jnp.concatenate(tiles[:4], axis=1),
         jnp.concatenate([tiles[4], jnp.zeros((8, 96), F32)], axis=1)], axis=0).astype(BF16)

    for slot, dz, dy, dx in others:
        pltpu.make_async_remote_copy(
            src_ref=m_send, dst_ref=m_recv.at[z, wide], send_sem=m_ss, recv_sem=m_rs,
            device_id=(wides[dy][dx], narrows[dz]), device_id_type=MESH).start()
    m_recv[z, wide] = m_send[...]

    def all_but_one(sem):
        ref = s_recv.at[pl.ds(1, 63)]
        pltpu.make_async_copy(ref, ref, sem).wait()

    all_but_one(m_rs)
    got = [m_recv[r].astype(F32) for r in range(4)]
    dense = block_turn([v[:, :8] for v in got])
    block = lax.broadcasted_iota(jnp.int32, (K, 8, 128), 2) // 32
    last = got[0][:, 8:]
    for r in range(1, 4):
        last = jnp.where(block == r, pltpu.roll(got[r][:, 8:], 32 * r, 2), last)
    for j, v in enumerate(dense + [last]):
        g_buf[core, pl.ds(128 * j, 128), :] = v.reshape(128, 128).astype(BF16)
    g_copy = pltpu.make_async_remote_copy(
        src_ref=g_buf.at[core], dst_ref=g_buf.at[core], send_sem=g_ss, recv_sem=g_rs,
        device_id=sibling, device_id_type=MESH)
    g_copy.start()

    def place(half):
        v = g_buf[half].astype(F32).reshape(80, 8, 128)
        turn = pltpu.roll(v, 4, 1)
        sw = jnp.where(lax.broadcasted_iota(jnp.int32, (80, 8, 128), 1) < 4, -turn, turn)
        c_half, s_half = phase[0, half], phase[1, half]
        at = pl.multiple_of(128 * half, 128)
        m_ref[:, pl.ds(at, 128)] = (c_half * v + s_half * sw).reshape(LANES, 128).astype(BF16)
        m_ref[:, pl.ds(256 + at, 128)] = (c_half * sw - s_half * v).reshape(LANES, 128).astype(BF16)

    place(core)

    all_but_one(s_ss)
    all_but_one(m_ss)
    for g in range(len(GROUPS)):
        c_copy(g).wait_send()
    g_copy.wait_recv()
    place(1 - core)
    g_copy.wait_send()


def spectra(plume, weight, t8, t4, e):
    vmem = pl.BlockSpec(memory_space=pltpu.VMEM)
    anywhere = pl.BlockSpec(memory_space=pl.ANY)
    dma = pltpu.SemaphoreType.DMA
    return pl.pallas_call(
        spectra_kernel,
        out_shape=jax.ShapeDtypeStruct((LANES, 2 * K * K), BF16),
        in_specs=[anywhere] * 5,
        out_specs=vmem,
        scratch_shapes=[
            pltpu.VMEM((C, YL, ZL, NX), BF16),
            pltpu.VMEM((32, 2 * C * C), F32),
            pltpu.VMEM((256, NX), BF16),
            pltpu.VMEM((128, NX), BF16),
            pltpu.VMEM((CELLS, 512), BF16),
            pltpu.VMEM((256, 8 * NX), BF16),
            pltpu.VMEM((128, 4 * NX), BF16),
            pltpu.VMEM((256, CELLS), BF16),
            pltpu.VMEM((2, LANES, 128), BF16),
            pltpu.VMEM((LANES, 128), BF16),
            pltpu.VMEM((LANES, 128), F32),
            pltpu.VMEM((4, 16, 16, 128), BF16),
            pltpu.VMEM((64, 16, 128), BF16),
            pltpu.VMEM((40, 32), F32),
            pltpu.VMEM((2 * C * C, 32), F32),
            pltpu.VMEM((16, 128), BF16),
            pltpu.VMEM((4, 16, 16, 128), BF16),
            pltpu.VMEM((2, LANES, 128), BF16),
            pltpu.VMEM((2, 2, 8, 128), F32),
            dma((3,)), dma((3,)), dma,
            dma((3,)), dma((3,)),
            dma, dma((4,)),
            dma, dma,
            dma, dma,
        ],
        compiler_params=pltpu.CompilerParams(
            collective_id=0, has_side_effects=True, vmem_limit_bytes=56 * 2**20),
        name="spectra",
    )(plume, weight, t8, t4, e)


CHUNKS = 4


def output_kernel(plume, m_ref, e_ref, lw_ref, bias_ref, xi_ref, out, x_buf, o_buf, b_buf, kron, rhs, in_sem, out_sem):
    yt = YL // CHUNKS

    def load(i):
        rows = pl.ds(i * yt, yt)
        return pltpu.make_async_copy(plume.at[:, rows], x_buf.at[:, rows], in_sem.at[i])

    def store(i):
        rows = pl.ds(i * yt, yt)
        return pltpu.make_async_copy(o_buf.at[:, rows], out.at[:, rows], out_sem.at[i])

    for i in range(CHUNKS):
        load(i).start()
    spread = jnp.where(
        lax.broadcasted_iota(jnp.int32, (320, C), 0) // 16 == lax.broadcasted_iota(jnp.int32, (320, C), 1),
        F32(1.0), F32(0.0)).astype(BF16)
    rows20 = jnp.dot(spread, lw_ref[...], preferred_element_type=F32).astype(BF16)
    across = jnp.where(
        lax.broadcasted_iota(jnp.int32, (C, 384), 1) // 16 == lax.broadcasted_iota(jnp.int32, (C, 384), 0),
        F32(1.0), F32(0.0)).astype(BF16)
    full = jnp.dot(rows20, across, preferred_element_type=F32)
    row = lax.broadcasted_iota(jnp.int32, (320, 384), 0)
    col = lax.broadcasted_iota(jnp.int32, (320, 384), 1)
    full = jnp.where((row % 16) == (col % 16), full, F32(0.0))
    own = (lax.broadcasted_iota(jnp.int32, (320, C), 0) // 16 == lax.broadcasted_iota(jnp.int32, (320, C), 1))
    bias = jnp.sum(jnp.where(own, bias_ref[...], F32(0.0)), axis=1, keepdims=True)
    b1 = bias.astype(BF16).astype(F32)
    b2 = (bias - b1).astype(BF16).astype(F32)
    b3 = bias - b1 - b2
    full = jnp.where(col == 320, b1, full)
    full = jnp.where(col == 321, b2, full)
    full = jnp.where(col == 322, b3, full)
    kron[...] = full.astype(BF16)
    for s in range(2):
        rhs[s, pl.ds(0, 128), :] = xi_ref[...]
        rhs[s, pl.ds(192, 64), :] = jnp.where(
            lax.broadcasted_iota(jnp.int32, (64, NX), 0) < 16, F32(1.0), F32(0.0)).astype(BF16)
    lane = lax.broadcasted_iota(jnp.int32, (16, 128), 1) % 4
    masks = [lane == k for k in range(4)]

    def chunk(i, _):
        load(i).wait()
        cells = yt * ZL
        b_buf[...] = lax.dot_general(
            e_ref[pl.ds(pl.multiple_of(i * cells, cells), cells), :], m_ref[...], CONTRACT_LANES,
            preferred_element_type=F32).astype(BF16)
        for q in range(cells // 16):
            y, z, s = i * yt + q // 2, (q % 2) * 16, q % 2
            xs = x_buf[:, y, pl.ds(z, 16), :].reshape(320, NX)
            rhs[s, pl.ds(128, 64), :] = xs[256:]
            parts = []
            for o in range(C):
                v = b_buf[pl.ds(16 * q, 16), pl.ds(128 * (o // 4), 128)]
                parts.append(jnp.where(masks[o % 4], v, jnp.zeros_like(v)))
            left = jnp.concatenate([jnp.concatenate(parts, 0), kron[:, pl.ds(256, 128)]], 1)
            acc = jnp.dot(kron[:, pl.ds(0, 256)], xs[:256], preferred_element_type=F32)
            acc = acc + jnp.dot(left, rhs[s], preferred_element_type=F32)
            half = 0.5 * acc
            y_out = half + half * lax.erf(acc * F32(math.sqrt(0.5)))
            o_buf[:, y, pl.ds(z, 16), :] = y_out.astype(BF16).reshape(C, 16, NX)
        store(i).start()
        return 0

    lax.fori_loop(0, CHUNKS, chunk, 0)
    for i in range(CHUNKS):
        store(i).wait()


def output(plume, m, e, lw, bias, xi):
    vmem = pl.BlockSpec(memory_space=pltpu.VMEM)
    anywhere = pl.BlockSpec(memory_space=pl.ANY)
    dma = pltpu.SemaphoreType.DMA
    return pl.pallas_call(
        output_kernel,
        out_shape=jax.ShapeDtypeStruct((C, YL, ZL, NX), BF16),
        in_specs=[anywhere] + [vmem] * 5,
        out_specs=anywhere,
        scratch_shapes=[
            pltpu.VMEM((C, YL, ZL, NX), BF16),
            pltpu.VMEM((C, YL, ZL, NX), BF16),
            pltpu.VMEM((CELLS // CHUNKS, LANES), BF16),
            pltpu.VMEM((320, 384), BF16),
            pltpu.VMEM((2, 256, NX), BF16),
            dma((CHUNKS,)), dma((CHUNKS,)),
        ],
        compiler_params=pltpu.CompilerParams(vmem_limit_bytes=56 * 2**20),
        name="output",
    )(plume, m, e, lw, bias, xi)


def on_device(plume, weight, linear_weight, channel_bias):
    t8, t4 = forward_table()
    e = jnp.asarray(mode_table())
    m = spectra(plume, weight.reshape(32, 2 * C * C), jnp.asarray(t8), jnp.asarray(t4), e)
    return output(plume, m, e, linear_weight, channel_bias.reshape(1, C), jnp.asarray(inverse_table()))


def solution(mesh):
    return jax.shard_map(
        on_device, mesh=mesh,
        in_specs=(P(None, "wide", "narrow", None), P("wide", "narrow", None, None), P(), P()),
        out_specs=P(None, "wide", "narrow", None), check_vma=False)
```

```python
import math

import jax
import jax.numpy as jnp
import ml_dtypes
import numpy as np
from jax import lax
from jax.experimental import pallas as pl
from jax.experimental.pallas import tpu as pltpu
from jax.sharding import PartitionSpec as P

MESH = pl.DeviceIdType.MESH
C, NX, NY, NZ, K = 20, 256, 512, 256, 16
YL, ZL = 32, 32
CELLS = YL * ZL
LANES = 2 * K * C
BF16, F32 = jnp.bfloat16, jnp.float32
GROUPS = ((0, 8, 0), (8, 8, 256), (16, 4, 512))
CONTRACT_LANES = (((1,), (1,)), ((), ()))


def np_bf16(a):
    return np.asarray(a, np.float32).astype(ml_dtypes.bfloat16)


def signed(m):
    return np.where(m < K // 2, m, m - K)


def x_tables():
    places, orders = np.arange(NX), np.arange(K)
    angles = np.mod(places[:, None] * orders[None, :], NX).astype(np.float32) * np.float32(2.0 * math.pi / NX)
    cos_tab, sin_tab = np.cos(angles), np.sin(angles)
    doubled = np.where(orders == 0, 1.0, 2.0).astype(np.float32)
    forward = np_bf16(np.stack([cos_tab, -sin_tab], -1))
    inverse = np_bf16(np.stack([cos_tab * doubled, -sin_tab * doubled], -1))
    return forward, inverse


def forward_table():
    forward = x_tables()[0].reshape(NX, 2 * K).T
    return np.repeat(forward, 8, axis=0), np.repeat(forward, 4, axis=0)


def inverse_table():
    inverse = x_tables()[1].reshape(NX, 2 * K).T
    return np.repeat(inverse, 4, axis=0)


def mode_order():
    core, z, j2, l = np.meshgrid(np.arange(2), np.arange(4), np.arange(2), np.arange(K), indexing="ij")
    return (2 * (2 * z + core) + j2).reshape(-1), l.reshape(-1)


def cell_angles():
    j, l = mode_order()
    fj, fl = signed(j), signed(l)
    y = np.mod(fj[:, None] * np.arange(YL)[None, :], NY) / NY
    z = np.mod(fl[:, None] * np.arange(ZL)[None, :], NZ) / NZ
    turns = y[:, :, None] + z[:, None, :]
    return 2.0 * math.pi * turns.reshape(K * K, CELLS)


def mode_table():
    angles = cell_angles().T
    return np_bf16(np.concatenate([np.cos(angles), np.sin(angles)], 1))


def offset_phase(wide, narrow):
    lane = lax.broadcasted_iota(jnp.int32, (8, 256), 1)
    l = lane % 16
    j = 2 * (2 * ((lane // 32) % 4) + lane // 128) + (lane // 16) % 2
    fj = jnp.where(j < K // 2, j, j - K)
    fl = jnp.where(l < K // 2, l, l - K)
    step = (fj * wide + 2 * fl * narrow) & 15
    cos_v = jnp.zeros((8, 256), F32)
    sin_v = jnp.zeros((8, 256), F32)
    for k in range(16):
        c, s = math.cos(math.pi * k / 8), math.sin(math.pi * k / 8)
        cos_v = jnp.where(step == k, F32(c), cos_v)
        sin_v = jnp.where(step == k, F32(s), sin_v)
    return cos_v, sin_v


def row_of(pair, c):
    if c < 8:
        return pair * 8 + c
    if c < 16:
        return 16 + pair * 8 + c - 8
    return 32 + pair * 4 + c - 16


def block_turn(tiles):
    shape = tiles[0].shape
    block = lax.broadcasted_iota(jnp.int32, shape, len(shape) - 1) // 32
    out = []
    for r in range(4):
        v = tiles[r]
        for b in range(4):
            if b != r:
                v = jnp.where(block == b, pltpu.roll(tiles[b], (32 * (b - r)) % 128, len(shape) - 1), v)
        out.append(v)
    return out


def spectra_kernel(
    plume, w_hbm, t8_hbm, t4_hbm, e_ref, lw_hbm, bias_hbm, xi_hbm,
    m_ref, x_buf, e_buf, kron, rhs,
    w_ref, t8_ref, t4_ref, lw_ref, bias_ref, xi_ref, tab8, tab4, a_buf, sib_send, sib_recv, mine, s_send, s_recv, q_buf, wt_buf, m_send, m_recv,
    g_buf, phase,
    in_sem, w_sem, e_sem, c_ss, c_rs, s_ss, s_rs, m_ss, m_rs, g_ss, g_rs,
):
    wide, narrow = lax.axis_index("wide"), lax.axis_index("narrow")
    y, x = lax.div(wide, 4), lax.rem(wide, 4)
    z, core = lax.div(narrow, 2), lax.rem(narrow, 2)
    sibling = (wide, narrow + 1 - 2 * core)
    e_copy = pltpu.make_async_copy(e_ref, e_buf, e_sem)
    small = [pltpu.make_async_copy(src, dst, w_sem.at[i]) for i, (src, dst) in enumerate(
        ((t8_hbm, t8_ref), (t4_hbm, t4_ref), (w_hbm, w_ref), (lw_hbm, lw_ref), (bias_hbm, bias_ref),
         (xi_hbm, xi_ref)))]
    for copy in small:
        copy.start()
    loads = []
    for g, (c0, nc, _) in enumerate(GROUPS):
        copy = pltpu.make_async_copy(plume.at[pl.ds(c0, nc)], x_buf.at[pl.ds(c0, nc)], in_sem.at[g])
        copy.start()
        loads.append(copy)
        if g == 0:
            e_copy.start()

    rows_of_chips = [4 * lax.rem(y + d, 4) for d in range(4)]
    places = [lax.rem(x + d, 4) for d in range(4)]
    wides = [[r + p for p in places] for r in rows_of_chips]
    layers = [lax.rem(z + d, 4) for d in range(4)]
    narrows = [2 * v + core for v in layers]
    far = (0, 1, 2, 1)
    others = sorted(
        [(16 * dz + 4 * dy + dx, dz, dy, dx) for dz in range(4) for dy in range(4) for dx in range(4)][1:],
        key=lambda v: (-(far[v[1]] + far[v[2]] + far[v[3]]), v))

    barrier = pltpu.get_barrier_semaphore()
    pl.semaphore_signal(barrier, inc=1, device_id=sibling, device_id_type=MESH)

    for _, dz, dy, dx in others:
        pl.semaphore_signal(barrier, inc=1, device_id=(wides[dy][dx], narrows[dz]), device_id_type=MESH)

    for copy in small[:2]:
        copy.wait()
    r8 = lax.broadcasted_iota(jnp.int32, (256, NX), 0) % 8
    r4 = lax.broadcasted_iota(jnp.int32, (128, NX), 0) % 4
    for c in range(8):
        tab8[:, pl.ds(NX * c, NX)] = jnp.where(r8 == c, t8_ref[...], jnp.zeros((), BF16))
    for c in range(4):
        tab4[:, pl.ds(NX * c, NX)] = jnp.where(r4 == c, t4_ref[...], jnp.zeros((), BF16))
    cos_v, sin_v = offset_phase(wide, narrow)
    for h in range(2):
        phase[0, h] = cos_v[:, 128 * h:128 * h + 128]
        phase[1, h] = sin_v[:, 128 * h:128 * h + 128]
    scale = F32(1.0 / math.sqrt(NX * NY * NZ))
    pc, ps = cos_v * scale, sin_v * scale

    def c_copy(g):
        c0, nc, row0 = GROUPS[g]
        rows = pl.ds(row0, 32 * nc)
        return pltpu.make_async_remote_copy(
            src_ref=sib_send.at[1 - core, rows], dst_ref=sib_recv.at[rows],
            send_sem=c_ss.at[g], recv_sem=c_rs.at[g], device_id=sibling, device_id_type=MESH)

    for g, (c0, nc, row0) in enumerate(GROUPS):
        loads[g].wait()
        table = tab8 if nc == 8 else tab4
        width = 32 * nc
        for r in range(4):
            rows = jnp.concatenate(
                [x_buf[c, pl.ds(8 * r, 8)].reshape(256, NX) for c in range(c0, c0 + nc)], axis=1)
            a_buf[pl.ds(0, width), pl.ds(256 * r, 256)] = lax.dot_general(
                table[...], rows, CONTRACT_LANES, preferred_element_type=F32).astype(BF16)
        if g == 0:
            e_copy.wait()
        turned = jnp.dot(a_buf[pl.ds(0, width), :], e_buf[...], preferred_element_type=F32)
        g_cos = turned[:, :256].reshape(width // 8, 8, 256)
        g_sin = turned[:, 256:].reshape(width // 8, 8, 256)
        rc = pc * g_cos - ps * g_sin
        rs = ps * g_cos + pc * g_sin
        if nc == 8:
            rc, rs = rc.reshape(K, 2, 8, 256), rs.reshape(K, 2, 8, 256)
            s = jnp.stack([rc[:, 0] + rs[:, 1], rc[:, 1] - rs[:, 0]], axis=1)
        else:
            first = lax.broadcasted_iota(jnp.int32, (K, 8, 256), 1) < 4
            turn = pltpu.roll(rs, 4, 1)
            s = rc + jnp.where(first, turn, -turn)
        s = s.reshape(width, 256)
        sib_send[0, pl.ds(row0, width), :] = s[:, :128].astype(BF16)
        sib_send[1, pl.ds(row0, width), :] = s[:, 128:].astype(BF16)
        mine[pl.ds(row0, width), :] = jnp.where(core == 0, s[:, :128], s[:, 128:])
        if g == 0:
            pl.semaphore_wait(barrier, 64)
        c_copy(g).start()

    for g in range(len(GROUPS)):
        c_copy(g).wait_recv()

    def both(g, size):
        _, nc, row0 = GROUPS[g]
        rows = pl.ds(row0, 32 * nc)
        return (mine[rows, :] + sib_recv[rows, :].astype(F32)).reshape(size)

    g0, g1, g2 = both(0, (K, 2, 8, 128)), both(1, (K, 2, 8, 128)), both(2, (K, 8, 128))
    dense = block_turn([g0[:, 0], g0[:, 1], g1[:, 0], g1[:, 1]])
    for r in range(4):
        rest = g2 if r == 0 else pltpu.roll(g2, 128 - 32 * r, 2)
        s_send[r] = jnp.concatenate([dense[r], rest], axis=1).astype(BF16)

    for slot, dz, dy, dx in others:
        pltpu.make_async_remote_copy(
            src_ref=s_send.at[layers[dz], wides[dy][dx]], dst_ref=s_recv.at[slot],
            send_sem=s_ss, recv_sem=s_rs.at[dz],
            device_id=(wides[dy][dx], narrows[dz]), device_id_type=MESH).start()

    def arrived(buf, sems, part):
        ref = buf.at[pl.ds(max(1, 16 * part), 16 if part else 15)]
        pltpu.make_async_copy(ref, ref, sems.at[part]).wait()

    for copy in small[2:]:
        copy.wait()
    for k in range(7):
        width = min(128, 2 * C * C - 128 * k)
        wt_buf[pl.ds(128 * k, width), :] = w_ref[:, pl.ds(128 * k, width)].T
    spread = jnp.where(
        lax.broadcasted_iota(jnp.int32, (320, C), 0) // 16 == lax.broadcasted_iota(jnp.int32, (320, C), 1),
        F32(1.0), F32(0.0)).astype(BF16)
    rows20 = jnp.dot(spread, lw_ref[...], preferred_element_type=F32).astype(BF16)
    across = jnp.where(
        lax.broadcasted_iota(jnp.int32, (C, 384), 1) // 16 == lax.broadcasted_iota(jnp.int32, (C, 384), 0),
        F32(1.0), F32(0.0)).astype(BF16)
    full = jnp.dot(rows20, across, preferred_element_type=F32)
    row = lax.broadcasted_iota(jnp.int32, (320, 384), 0)
    col = lax.broadcasted_iota(jnp.int32, (320, 384), 1)
    full = jnp.where((row % 16) == (col % 16), full, F32(0.0))
    own = (lax.broadcasted_iota(jnp.int32, (320, C), 0) // 16 == lax.broadcasted_iota(jnp.int32, (320, C), 1))
    bias = jnp.sum(jnp.where(own, bias_ref[...], F32(0.0)), axis=1, keepdims=True)
    b1 = bias.astype(BF16).astype(F32)
    b2 = (bias - b1).astype(BF16).astype(F32)
    b3 = bias - b1 - b2
    full = jnp.where(col == 320, b1, full)
    full = jnp.where(col == 321, b2, full)
    full = jnp.where(col == 322, b3, full)
    kron[...] = full.astype(BF16)
    for s in range(2):
        rhs[s, pl.ds(0, 128), :] = xi_ref[...]
        rhs[s, pl.ds(192, 64), :] = jnp.where(
            lax.broadcasted_iota(jnp.int32, (64, NX), 0) < 16, F32(1.0), F32(0.0)).astype(BF16)
    total = s_send[z, wide].astype(F32)
    for part in (0, 1, 3, 2):
        first = max(1, 16 * part)
        arrived(s_recv, s_rs, part)
        total = total + jnp.sum(s_recv[pl.ds(first, 16 * part + 16 - first)].astype(F32), axis=0)
    for t in range(4):
        v = total[0:8] if t == 0 else pltpu.roll(total[0:8], 128 - 32 * t, 1)
        q_buf[pl.ds(8 * t, 8), :] = v[:, :32]
    q_buf[pl.ds(32, 8), :] = total[8:16, :32]

    out_re = jnp.zeros((C, 32), F32)
    out_im = jnp.zeros((C, 32), F32)
    for c in range(C):
        s_re = q_buf[pl.ds(row_of(0, c), 1), :]
        s_im = q_buf[pl.ds(row_of(1, c), 1), :]
        w_re = wt_buf[pl.ds(C * c, C), :]
        w_im = wt_buf[pl.ds(C * C + C * c, C), :]
        out_re = out_re + (w_re * s_re - w_im * s_im)
        out_im = out_im + (w_re * s_im + w_im * s_re)
    tiles = [jnp.concatenate([out_re[4 * j:4 * j + 4], out_im[4 * j:4 * j + 4]], axis=0) for j in range(5)]
    m_send[...] = jnp.concatenate(
        [jnp.concatenate(tiles[:4], axis=1),
         jnp.concatenate([tiles[4], jnp.zeros((8, 96), F32)], axis=1)], axis=0).astype(BF16)

    for slot, dz, dy, dx in others:
        pltpu.make_async_remote_copy(
            src_ref=m_send, dst_ref=m_recv.at[z, wide], send_sem=m_ss, recv_sem=m_rs,
            device_id=(wides[dy][dx], narrows[dz]), device_id_type=MESH).start()
    m_recv[z, wide] = m_send[...]

    def all_but_one(sem):
        ref = s_recv.at[pl.ds(1, 63)]
        pltpu.make_async_copy(ref, ref, sem).wait()

    all_but_one(m_rs)
    got = [m_recv[r].astype(F32) for r in range(4)]
    dense = block_turn([v[:, :8] for v in got])
    block = lax.broadcasted_iota(jnp.int32, (K, 8, 128), 2) // 32
    last = got[0][:, 8:]
    for r in range(1, 4):
        last = jnp.where(block == r, pltpu.roll(got[r][:, 8:], 32 * r, 2), last)
    for j, v in enumerate(dense + [last]):
        g_buf[core, pl.ds(128 * j, 128), :] = v.reshape(128, 128).astype(BF16)
    g_copy = pltpu.make_async_remote_copy(
        src_ref=g_buf.at[core], dst_ref=g_buf.at[core], send_sem=g_ss, recv_sem=g_rs,
        device_id=sibling, device_id_type=MESH)
    g_copy.start()

    def place(half):
        v = g_buf[half].astype(F32).reshape(80, 8, 128)
        turn = pltpu.roll(v, 4, 1)
        sw = jnp.where(lax.broadcasted_iota(jnp.int32, (80, 8, 128), 1) < 4, -turn, turn)
        c_half, s_half = phase[0, half], phase[1, half]
        at = pl.multiple_of(128 * half, 128)
        m_ref[:, pl.ds(at, 128)] = (c_half * v + s_half * sw).reshape(LANES, 128).astype(BF16)
        m_ref[:, pl.ds(256 + at, 128)] = (c_half * sw - s_half * v).reshape(LANES, 128).astype(BF16)

    place(core)

    all_but_one(s_ss)
    all_but_one(m_ss)
    for g in range(len(GROUPS)):
        c_copy(g).wait_send()
    g_copy.wait_recv()
    place(1 - core)
    g_copy.wait_send()


def spectra(plume, weight, t8, t4, e, lw, bias, xi):
    vmem = pl.BlockSpec(memory_space=pltpu.VMEM)
    anywhere = pl.BlockSpec(memory_space=pl.ANY)
    dma = pltpu.SemaphoreType.DMA
    return pl.pallas_call(
        spectra_kernel,
        out_shape=(
            pltpu.VMEM((LANES, 2 * K * K), BF16),
            pltpu.VMEM((C, YL, ZL, NX), BF16),
            pltpu.VMEM((CELLS, 512), BF16),
            pltpu.VMEM((320, 384), BF16),
            pltpu.VMEM((2, 256, NX), BF16),
        ),
        in_specs=[anywhere] * 8,
        out_specs=(vmem,) * 5,
        scratch_shapes=[
            pltpu.VMEM((32, 2 * C * C), F32),
            pltpu.VMEM((256, NX), BF16),
            pltpu.VMEM((128, NX), BF16),
            pltpu.VMEM((C, C), BF16),
            pltpu.VMEM((1, C), F32),
            pltpu.VMEM((128, NX), BF16),
            pltpu.VMEM((256, 8 * NX), BF16),
            pltpu.VMEM((128, 4 * NX), BF16),
            pltpu.VMEM((256, CELLS), BF16),
            pltpu.VMEM((2, LANES, 128), BF16),
            pltpu.VMEM((LANES, 128), BF16),
            pltpu.VMEM((LANES, 128), F32),
            pltpu.VMEM((4, 16, 16, 128), BF16),
            pltpu.VMEM((64, 16, 128), BF16),
            pltpu.VMEM((40, 32), F32),
            pltpu.VMEM((2 * C * C, 32), F32),
            pltpu.VMEM((16, 128), BF16),
            pltpu.VMEM((4, 16, 16, 128), BF16),
            pltpu.VMEM((2, LANES, 128), BF16),
            pltpu.VMEM((2, 2, 8, 128), F32),
            dma((3,)), dma((6,)), dma,
            dma((3,)), dma((3,)),
            dma, dma((4,)),
            dma, dma,
            dma, dma,
        ],
        compiler_params=pltpu.CompilerParams(
            collective_id=0, has_side_effects=True, vmem_limit_bytes=51 * 2**20),
        name="spectra",
    )(plume, weight, t8, t4, e, lw, bias, xi)


CHUNKS = 4


def output_kernel(m_ref, x_buf, e_ref, kron, rhs, out, o_buf, b_buf, out_sem):
    yt = YL // CHUNKS

    def store(i):
        rows = pl.ds(i * yt, yt)
        return pltpu.make_async_copy(o_buf.at[:, rows], out.at[:, rows], out_sem.at[i])

    lane = lax.broadcasted_iota(jnp.int32, (16, 128), 1) % 4
    masks = [lane == k for k in range(4)]

    def chunk(i, _):
        cells = yt * ZL
        b_buf[...] = lax.dot_general(
            e_ref[pl.ds(pl.multiple_of(i * cells, cells), cells), :], m_ref[...], CONTRACT_LANES,
            preferred_element_type=F32).astype(BF16)
        for q in range(cells // 16):
            y, z, s = i * yt + q // 2, (q % 2) * 16, q % 2
            xs = x_buf[:, y, pl.ds(z, 16), :].reshape(320, NX)
            rhs[s, pl.ds(128, 64), :] = xs[256:]
            parts = []
            for o in range(C):
                v = b_buf[pl.ds(16 * q, 16), pl.ds(128 * (o // 4), 128)]
                parts.append(jnp.where(masks[o % 4], v, jnp.zeros_like(v)))
            left = jnp.concatenate([jnp.concatenate(parts, 0), kron[:, pl.ds(256, 128)]], 1)
            acc = jnp.dot(kron[:, pl.ds(0, 256)], xs[:256], preferred_element_type=F32)
            acc = acc + jnp.dot(left, rhs[s], preferred_element_type=F32)
            half = 0.5 * acc
            y_out = half + half * lax.erf(acc * F32(math.sqrt(0.5)))
            o_buf[:, y, pl.ds(z, 16), :] = y_out.astype(BF16).reshape(C, 16, NX)
        store(i).start()
        return 0

    lax.fori_loop(0, CHUNKS, chunk, 0)
    for i in range(CHUNKS):
        store(i).wait()


def output(m, x, e, kron, rhs):
    vmem = pl.BlockSpec(memory_space=pltpu.VMEM)
    return pl.pallas_call(
        output_kernel,
        out_shape=jax.ShapeDtypeStruct((C, YL, ZL, NX), BF16),
        in_specs=[vmem] * 5,
        out_specs=pl.BlockSpec(memory_space=pltpu.HBM),
        scratch_shapes=[
            pltpu.VMEM((C, YL, ZL, NX), BF16),
            pltpu.VMEM((CELLS // CHUNKS, LANES), BF16),
            pltpu.SemaphoreType.DMA((CHUNKS,)),
        ],
        compiler_params=pltpu.CompilerParams(vmem_limit_bytes=16 * 2**20),
        name="output",
    )(m, x, e, kron, rhs)


def on_device(plume, weight, linear_weight, channel_bias):
    t8, t4 = forward_table()
    return output(*spectra(
        plume, weight.reshape(32, 2 * C * C), jnp.asarray(t8), jnp.asarray(t4), jnp.asarray(mode_table()),
        linear_weight, channel_bias.reshape(1, C), jnp.asarray(inverse_table())))


def solution(mesh):
    return jax.shard_map(
        on_device, mesh=mesh,
        in_specs=(P(None, "wide", "narrow", None), P("wide", "narrow", None, None), P(), P()),
        out_specs=P(None, "wide", "narrow", None), check_vma=False)
```

```python
import math

import jax
import jax.numpy as jnp
import ml_dtypes
import numpy as np
from jax import lax
from jax.experimental import pallas as pl
from jax.experimental.pallas import tpu as pltpu
from jax.sharding import PartitionSpec as P

MESH = pl.DeviceIdType.MESH
C, NX, NY, NZ, K = 20, 256, 512, 256, 16
YL, ZL = 32, 32
CELLS = YL * ZL
LANES = 2 * K * C
BF16, F32 = jnp.bfloat16, jnp.float32
GROUPS = ((0, 8, 0), (8, 8, 256), (16, 4, 512))
CONTRACT_LANES = (((1,), (1,)), ((), ()))


def np_bf16(a):
    return np.asarray(a, np.float32).astype(ml_dtypes.bfloat16)


def signed(m):
    return np.where(m < K // 2, m, m - K)


def x_tables():
    places, orders = np.arange(NX), np.arange(K)
    angles = np.mod(places[:, None] * orders[None, :], NX).astype(np.float32) * np.float32(2.0 * math.pi / NX)
    cos_tab, sin_tab = np.cos(angles), np.sin(angles)
    doubled = np.where(orders == 0, 1.0, 2.0).astype(np.float32)
    forward = np_bf16(np.stack([cos_tab, -sin_tab], -1))
    inverse = np_bf16(np.stack([cos_tab * doubled, -sin_tab * doubled], -1))
    return forward, inverse


def forward_table():
    forward = x_tables()[0].reshape(NX, 2 * K).T
    return np.repeat(forward, 8, axis=0), np.repeat(forward, 4, axis=0)


def inverse_table():
    inverse = x_tables()[1].reshape(NX, 2 * K).T
    return np.repeat(inverse, 4, axis=0)


def mode_order():
    core, z, j2, l = np.meshgrid(np.arange(2), np.arange(4), np.arange(2), np.arange(K), indexing="ij")
    return (2 * (2 * z + core) + j2).reshape(-1), l.reshape(-1)


def cell_angles():
    j, l = mode_order()
    fj, fl = signed(j), signed(l)
    y = np.mod(fj[:, None] * np.arange(YL)[None, :], NY) / NY
    z = np.mod(fl[:, None] * np.arange(ZL)[None, :], NZ) / NZ
    turns = y[:, :, None] + z[:, None, :]
    return 2.0 * math.pi * turns.reshape(K * K, CELLS)


def mode_table():
    angles = cell_angles().T
    return np_bf16(np.concatenate([np.cos(angles), np.sin(angles)], 1))


def offset_phase(wide, narrow):
    lane = lax.broadcasted_iota(jnp.int32, (8, 256), 1)
    l = lane % 16
    j = 2 * (2 * ((lane // 32) % 4) + lane // 128) + (lane // 16) % 2
    fj = jnp.where(j < K // 2, j, j - K)
    fl = jnp.where(l < K // 2, l, l - K)
    step = (fj * wide + 2 * fl * narrow) & 15
    cos_v = jnp.zeros((8, 256), F32)
    sin_v = jnp.zeros((8, 256), F32)
    for k in range(16):
        c, s = math.cos(math.pi * k / 8), math.sin(math.pi * k / 8)
        cos_v = jnp.where(step == k, F32(c), cos_v)
        sin_v = jnp.where(step == k, F32(s), sin_v)
    return cos_v, sin_v


def row_of(pair, c):
    if c < 8:
        return pair * 8 + c
    if c < 16:
        return 16 + pair * 8 + c - 8
    return 32 + pair * 4 + c - 16


def block_turn(tiles):
    shape = tiles[0].shape
    block = lax.broadcasted_iota(jnp.int32, shape, len(shape) - 1) // 32
    out = []
    for r in range(4):
        v = tiles[r]
        for b in range(4):
            if b != r:
                v = jnp.where(block == b, pltpu.roll(tiles[b], (32 * (b - r)) % 128, len(shape) - 1), v)
        out.append(v)
    return out


def spectra_kernel(
    plume, w_hbm, t8_hbm, t4_hbm, e_ref, lw_hbm, bias_hbm, xi_hbm,
    m_ref, x_buf, e_buf, kron, rhs,
    w_ref, t8_ref, t4_ref, lw_ref, bias_ref, xi_ref, tab8, tab4, a_buf, sib_send, sib_recv, mine, s_send, s_recv, q_buf, wt_buf, m_send, m_recv,
    g_buf, phase,
    in_sem, w_sem, e_sem, c_ss, c_rs, s_ss, s_rs, m_ss, m_rs, g_ss, g_rs,
):
    wide, narrow = lax.axis_index("wide"), lax.axis_index("narrow")
    y, x = lax.div(wide, 4), lax.rem(wide, 4)
    z, core = lax.div(narrow, 2), lax.rem(narrow, 2)
    sibling = (wide, narrow + 1 - 2 * core)
    e_copy = pltpu.make_async_copy(e_ref, e_buf, e_sem)
    small = [pltpu.make_async_copy(src, dst, w_sem.at[i]) for i, (src, dst) in enumerate(
        ((t8_hbm, t8_ref), (t4_hbm, t4_ref), (w_hbm, w_ref), (lw_hbm, lw_ref), (bias_hbm, bias_ref),
         (xi_hbm, xi_ref)))]
    for copy in small[:2]:
        copy.start()
    loads = []
    for g, (c0, nc, _) in enumerate(GROUPS):
        copy = pltpu.make_async_copy(plume.at[pl.ds(c0, nc)], x_buf.at[pl.ds(c0, nc)], in_sem.at[g])
        copy.start()
        loads.append(copy)
        if g == 0:
            e_copy.start()
    for copy in small[2:]:
        copy.start()

    rows_of_chips = [4 * lax.rem(y + d, 4) for d in range(4)]
    places = [lax.rem(x + d, 4) for d in range(4)]
    wides = [[r + p for p in places] for r in rows_of_chips]
    layers = [lax.rem(z + d, 4) for d in range(4)]
    narrows = [2 * v + core for v in layers]
    far = (0, 1, 2, 1)
    others = sorted(
        [(16 * dz + 4 * dy + dx, dz, dy, dx) for dz in range(4) for dy in range(4) for dx in range(4)][1:],
        key=lambda v: (-(far[v[1]] + far[v[2]] + far[v[3]]), v))

    barrier = pltpu.get_barrier_semaphore()
    pl.semaphore_signal(barrier, inc=1, device_id=sibling, device_id_type=MESH)

    for _, dz, dy, dx in others:
        pl.semaphore_signal(barrier, inc=1, device_id=(wides[dy][dx], narrows[dz]), device_id_type=MESH)

    for copy in small[:2]:
        copy.wait()
    r8 = lax.broadcasted_iota(jnp.int32, (256, NX), 0) % 8
    r4 = lax.broadcasted_iota(jnp.int32, (128, NX), 0) % 4
    for c in range(8):
        tab8[:, pl.ds(NX * c, NX)] = jnp.where(r8 == c, t8_ref[...], jnp.zeros((), BF16))
    for c in range(4):
        tab4[:, pl.ds(NX * c, NX)] = jnp.where(r4 == c, t4_ref[...], jnp.zeros((), BF16))
    cos_v, sin_v = offset_phase(wide, narrow)
    for h in range(2):
        phase[0, h] = cos_v[:, 128 * h:128 * h + 128]
        phase[1, h] = sin_v[:, 128 * h:128 * h + 128]
    scale = F32(1.0 / math.sqrt(NX * NY * NZ))
    pc, ps = cos_v * scale, sin_v * scale

    def c_copy(g):
        c0, nc, row0 = GROUPS[g]
        rows = pl.ds(row0, 32 * nc)
        return pltpu.make_async_remote_copy(
            src_ref=sib_send.at[1 - core, rows], dst_ref=sib_recv.at[rows],
            send_sem=c_ss.at[g], recv_sem=c_rs.at[g], device_id=sibling, device_id_type=MESH)

    for g, (c0, nc, row0) in enumerate(GROUPS):
        loads[g].wait()
        table = tab8 if nc == 8 else tab4
        width = 32 * nc
        for r in range(4):
            rows = jnp.concatenate(
                [x_buf[c, pl.ds(8 * r, 8)].reshape(256, NX) for c in range(c0, c0 + nc)], axis=1)
            a_buf[pl.ds(0, width), pl.ds(256 * r, 256)] = lax.dot_general(
                table[...], rows, CONTRACT_LANES, preferred_element_type=F32).astype(BF16)
        if g == 0:
            e_copy.wait()
        turned = jnp.dot(a_buf[pl.ds(0, width), :], e_buf[...], preferred_element_type=F32)
        g_cos = turned[:, :256].reshape(width // 8, 8, 256)
        g_sin = turned[:, 256:].reshape(width // 8, 8, 256)
        rc = pc * g_cos - ps * g_sin
        rs = ps * g_cos + pc * g_sin
        if nc == 8:
            rc, rs = rc.reshape(K, 2, 8, 256), rs.reshape(K, 2, 8, 256)
            s = jnp.stack([rc[:, 0] + rs[:, 1], rc[:, 1] - rs[:, 0]], axis=1)
        else:
            first = lax.broadcasted_iota(jnp.int32, (K, 8, 256), 1) < 4
            turn = pltpu.roll(rs, 4, 1)
            s = rc + jnp.where(first, turn, -turn)
        s = s.reshape(width, 256)
        sib_send[0, pl.ds(row0, width), :] = s[:, :128].astype(BF16)
        sib_send[1, pl.ds(row0, width), :] = s[:, 128:].astype(BF16)
        mine[pl.ds(row0, width), :] = jnp.where(core == 0, s[:, :128], s[:, 128:])
        if g == 0:
            pl.semaphore_wait(barrier, 64)
        c_copy(g).start()

    for g in range(len(GROUPS)):
        c_copy(g).wait_recv()

    def both(g, size):
        _, nc, row0 = GROUPS[g]
        rows = pl.ds(row0, 32 * nc)
        return (mine[rows, :] + sib_recv[rows, :].astype(F32)).reshape(size)

    g0, g1, g2 = both(0, (K, 2, 8, 128)), both(1, (K, 2, 8, 128)), both(2, (K, 8, 128))
    dense = block_turn([g0[:, 0], g0[:, 1], g1[:, 0], g1[:, 1]])
    for r in range(4):
        rest = g2 if r == 0 else pltpu.roll(g2, 128 - 32 * r, 2)
        s_send[r] = jnp.concatenate([dense[r], rest], axis=1).astype(BF16)

    for slot, dz, dy, dx in others:
        pltpu.make_async_remote_copy(
            src_ref=s_send.at[layers[dz], wides[dy][dx]], dst_ref=s_recv.at[slot],
            send_sem=s_ss, recv_sem=s_rs.at[dz],
            device_id=(wides[dy][dx], narrows[dz]), device_id_type=MESH).start()

    def arrived(buf, sems, part):
        ref = buf.at[pl.ds(max(1, 16 * part), 16 if part else 15)]
        pltpu.make_async_copy(ref, ref, sems.at[part]).wait()

    for copy in small[2:]:
        copy.wait()
    for k in range(7):
        width = min(128, 2 * C * C - 128 * k)
        wt_buf[pl.ds(128 * k, width), :] = w_ref[:, pl.ds(128 * k, width)].T
    spread = jnp.where(
        lax.broadcasted_iota(jnp.int32, (320, C), 0) // 16 == lax.broadcasted_iota(jnp.int32, (320, C), 1),
        F32(1.0), F32(0.0)).astype(BF16)
    rows20 = jnp.dot(spread, lw_ref[...], preferred_element_type=F32).astype(BF16)
    across = jnp.where(
        lax.broadcasted_iota(jnp.int32, (C, 384), 1) // 16 == lax.broadcasted_iota(jnp.int32, (C, 384), 0),
        F32(1.0), F32(0.0)).astype(BF16)
    full = jnp.dot(rows20, across, preferred_element_type=F32)
    row = lax.broadcasted_iota(jnp.int32, (320, 384), 0)
    col = lax.broadcasted_iota(jnp.int32, (320, 384), 1)
    full = jnp.where((row % 16) == (col % 16), full, F32(0.0))
    own = (lax.broadcasted_iota(jnp.int32, (320, C), 0) // 16 == lax.broadcasted_iota(jnp.int32, (320, C), 1))
    bias = jnp.sum(jnp.where(own, bias_ref[...], F32(0.0)), axis=1, keepdims=True)
    b1 = bias.astype(BF16).astype(F32)
    b2 = (bias - b1).astype(BF16).astype(F32)
    b3 = bias - b1 - b2
    full = jnp.where(col == 320, b1, full)
    full = jnp.where(col == 321, b2, full)
    full = jnp.where(col == 322, b3, full)
    kron[...] = full.astype(BF16)
    for s in range(2):
        rhs[s, pl.ds(0, 128), :] = xi_ref[...]
        rhs[s, pl.ds(192, 64), :] = jnp.where(
            lax.broadcasted_iota(jnp.int32, (64, NX), 0) < 16, F32(1.0), F32(0.0)).astype(BF16)
    total = s_send[z, wide].astype(F32)
    for part in (0, 1, 3, 2):
        first = max(1, 16 * part)
        arrived(s_recv, s_rs, part)
        total = total + jnp.sum(s_recv[pl.ds(first, 16 * part + 16 - first)].astype(F32), axis=0)
    for t in range(4):
        v = total[0:8] if t == 0 else pltpu.roll(total[0:8], 128 - 32 * t, 1)
        q_buf[pl.ds(8 * t, 8), :] = v[:, :32]
    q_buf[pl.ds(32, 8), :] = total[8:16, :32]

    out_re = jnp.zeros((C, 32), F32)
    out_im = jnp.zeros((C, 32), F32)
    for c in range(C):
        s_re = q_buf[pl.ds(row_of(0, c), 1), :]
        s_im = q_buf[pl.ds(row_of(1, c), 1), :]
        w_re = wt_buf[pl.ds(C * c, C), :]
        w_im = wt_buf[pl.ds(C * C + C * c, C), :]
        out_re = out_re + (w_re * s_re - w_im * s_im)
        out_im = out_im + (w_re * s_im + w_im * s_re)
    tiles = [jnp.concatenate([out_re[4 * j:4 * j + 4], out_im[4 * j:4 * j + 4]], axis=0) for j in range(5)]
    m_send[...] = jnp.concatenate(
        [jnp.concatenate(tiles[:4], axis=1),
         jnp.concatenate([tiles[4], jnp.zeros((8, 96), F32)], axis=1)], axis=0).astype(BF16)

    for slot, dz, dy, dx in others:
        pltpu.make_async_remote_copy(
            src_ref=m_send, dst_ref=m_recv.at[z, wide], send_sem=m_ss, recv_sem=m_rs,
            device_id=(wides[dy][dx], narrows[dz]), device_id_type=MESH).start()
    m_recv[z, wide] = m_send[...]

    def all_but_one(sem):
        ref = s_recv.at[pl.ds(1, 63)]
        pltpu.make_async_copy(ref, ref, sem).wait()

    all_but_one(m_rs)
    got = [m_recv[r].astype(F32) for r in range(4)]
    dense = block_turn([v[:, :8] for v in got])
    block = lax.broadcasted_iota(jnp.int32, (K, 8, 128), 2) // 32
    last = got[0][:, 8:]
    for r in range(1, 4):
        last = jnp.where(block == r, pltpu.roll(got[r][:, 8:], 32 * r, 2), last)
    def g_copy(j):
        rows = pl.ds(128 * j, 128)
        return pltpu.make_async_remote_copy(
            src_ref=g_buf.at[core, rows], dst_ref=g_buf.at[core, rows], send_sem=g_ss.at[j], recv_sem=g_rs.at[j],
            device_id=sibling, device_id_type=MESH)

    for j, v in enumerate(dense + [last]):
        g_buf[core, pl.ds(128 * j, 128), :] = v.reshape(128, 128).astype(BF16)
        g_copy(j).start()

    def place(half):
        v = g_buf[half].astype(F32).reshape(80, 8, 128)
        turn = pltpu.roll(v, 4, 1)
        sw = jnp.where(lax.broadcasted_iota(jnp.int32, (80, 8, 128), 1) < 4, -turn, turn)
        c_half, s_half = phase[0, half], phase[1, half]
        at = pl.multiple_of(128 * half, 128)
        m_ref[:, pl.ds(at, 128)] = (c_half * v + s_half * sw).reshape(LANES, 128).astype(BF16)
        m_ref[:, pl.ds(256 + at, 128)] = (c_half * sw - s_half * v).reshape(LANES, 128).astype(BF16)

    place(core)

    all_but_one(s_ss)
    all_but_one(m_ss)
    for g in range(len(GROUPS)):
        c_copy(g).wait_send()
    for j in range(5):
        g_copy(j).wait_recv()
    place(1 - core)
    for j in range(5):
        g_copy(j).wait_send()


def spectra(plume, weight, t8, t4, e, lw, bias, xi):
    vmem = pl.BlockSpec(memory_space=pltpu.VMEM)
    anywhere = pl.BlockSpec(memory_space=pl.ANY)
    dma = pltpu.SemaphoreType.DMA
    return pl.pallas_call(
        spectra_kernel,
        out_shape=(
            pltpu.VMEM((LANES, 2 * K * K), BF16),
            pltpu.VMEM((C, YL, ZL, NX), BF16),
            pltpu.VMEM((CELLS, 512), BF16),
            pltpu.VMEM((320, 384), BF16),
            pltpu.VMEM((2, 256, NX), BF16),
        ),
        in_specs=[anywhere] * 8,
        out_specs=(vmem,) * 5,
        scratch_shapes=[
            pltpu.VMEM((32, 2 * C * C), F32),
            pltpu.VMEM((256, NX), BF16),
            pltpu.VMEM((128, NX), BF16),
            pltpu.VMEM((C, C), BF16),
            pltpu.VMEM((1, C), F32),
            pltpu.VMEM((128, NX), BF16),
            pltpu.VMEM((256, 8 * NX), BF16),
            pltpu.VMEM((128, 4 * NX), BF16),
            pltpu.VMEM((256, CELLS), BF16),
            pltpu.VMEM((2, LANES, 128), BF16),
            pltpu.VMEM((LANES, 128), BF16),
            pltpu.VMEM((LANES, 128), F32),
            pltpu.VMEM((4, 16, 16, 128), BF16),
            pltpu.VMEM((64, 16, 128), BF16),
            pltpu.VMEM((40, 32), F32),
            pltpu.VMEM((2 * C * C, 32), F32),
            pltpu.VMEM((16, 128), BF16),
            pltpu.VMEM((4, 16, 16, 128), BF16),
            pltpu.VMEM((2, LANES, 128), BF16),
            pltpu.VMEM((2, 2, 8, 128), F32),
            dma((3,)), dma((6,)), dma,
            dma((3,)), dma((3,)),
            dma, dma((4,)),
            dma, dma,
            dma((5,)), dma((5,)),
        ],
        compiler_params=pltpu.CompilerParams(
            collective_id=0, has_side_effects=True, vmem_limit_bytes=51 * 2**20),
        name="spectra",
    )(plume, weight, t8, t4, e, lw, bias, xi)


CHUNKS = 4
STORED = 2


def output_kernel(m_ref, x_buf, e_ref, kron, rhs, out, o_buf, b_buf, out_sem):
    yt = YL // CHUNKS

    def store(i):
        rows = pl.ds(i * STORED, STORED)
        return pltpu.make_async_copy(o_buf.at[:, rows], out.at[:, rows], out_sem.at[i])

    lane = lax.broadcasted_iota(jnp.int32, (16, 128), 1) % 4
    masks = [lane == k for k in range(4)]

    def chunk(i, _):
        cells = yt * ZL
        b_buf[...] = lax.dot_general(
            e_ref[pl.ds(pl.multiple_of(i * cells, cells), cells), :], m_ref[...], CONTRACT_LANES,
            preferred_element_type=F32).astype(BF16)
        for q in range(cells // 16):
            y, z, s = i * yt + q // 2, (q % 2) * 16, q % 2
            xs = x_buf[:, y, pl.ds(z, 16), :].reshape(320, NX)
            parts = []
            for o in range(C):
                v = b_buf[pl.ds(16 * q, 16), pl.ds(128 * (o // 4), 128)]
                parts.append(jnp.where(masks[o % 4], v, jnp.zeros_like(v)))
            left = jnp.concatenate([jnp.concatenate(parts, 0), kron[:, pl.ds(256, 128)]], 1)
            left = jnp.concatenate([kron[:, pl.ds(0, 256)], left], 1)
            right = jnp.concatenate(
                [xs[:256], rhs[0, pl.ds(0, 128), :], xs[256:], rhs[0, pl.ds(192, 64), :]], 0)
            acc = jnp.dot(left, right, preferred_element_type=F32)
            half = 0.5 * acc
            y_out = half + half * lax.erf(acc * F32(math.sqrt(0.5)))
            o_buf[:, y, pl.ds(z, 16), :] = y_out.astype(BF16).reshape(C, 16, NX)
            if q % (2 * STORED) == 2 * STORED - 1:
                store(i * (yt // STORED) + q // (2 * STORED)).start()
        return 0

    lax.fori_loop(0, CHUNKS, chunk, 0)
    for i in range(YL // STORED):
        store(i).wait()


def output(m, x, e, kron, rhs):
    vmem = pl.BlockSpec(memory_space=pltpu.VMEM)
    return pl.pallas_call(
        output_kernel,
        out_shape=jax.ShapeDtypeStruct((C, YL, ZL, NX), BF16),
        in_specs=[vmem] * 5,
        out_specs=pl.BlockSpec(memory_space=pltpu.HBM),
        scratch_shapes=[
            pltpu.VMEM((C, YL, ZL, NX), BF16),
            pltpu.VMEM((CELLS // CHUNKS, LANES), BF16),
            pltpu.SemaphoreType.DMA((YL // STORED,)),
        ],
        compiler_params=pltpu.CompilerParams(vmem_limit_bytes=16 * 2**20),
        name="output",
    )(m, x, e, kron, rhs)


def on_device(plume, weight, linear_weight, channel_bias):
    t8, t4 = forward_table()
    return output(*spectra(
        plume, weight.reshape(32, 2 * C * C), jnp.asarray(t8), jnp.asarray(t4), jnp.asarray(mode_table()),
        linear_weight, channel_bias.reshape(1, C), jnp.asarray(inverse_table())))


def solution(mesh):
    return jax.shard_map(
        on_device, mesh=mesh,
        in_specs=(P(None, "wide", "narrow", None), P("wide", "narrow", None, None), P(), P()),
        out_specs=P(None, "wide", "narrow", None), check_vma=False)
```

```python
import math

import jax
import jax.numpy as jnp
import ml_dtypes
import numpy as np
from jax import lax
from jax.experimental import pallas as pl
from jax.experimental.pallas import tpu as pltpu
from jax.sharding import PartitionSpec as P

MESH = pl.DeviceIdType.MESH
C, NX, NY, NZ, K = 20, 256, 512, 256, 16
YL, ZL = 32, 32
CELLS = YL * ZL
LANES = 2 * K * C
BF16, F32 = jnp.bfloat16, jnp.float32
GROUPS = ((0, 8, 0), (8, 8, 256), (16, 4, 512))
CONTRACT_LANES = (((1,), (1,)), ((), ()))


def np_bf16(a):
    return np.asarray(a, np.float32).astype(ml_dtypes.bfloat16)


def signed(m):
    return np.where(m < K // 2, m, m - K)


def x_tables():
    places, orders = np.arange(NX), np.arange(K)
    angles = np.mod(places[:, None] * orders[None, :], NX).astype(np.float32) * np.float32(2.0 * math.pi / NX)
    cos_tab, sin_tab = np.cos(angles), np.sin(angles)
    doubled = np.where(orders == 0, 1.0, 2.0).astype(np.float32)
    forward = np_bf16(np.stack([cos_tab, -sin_tab], -1))
    inverse = np_bf16(np.stack([cos_tab * doubled, -sin_tab * doubled], -1))
    return forward, inverse


def forward_table():
    forward = x_tables()[0].reshape(NX, 2 * K).T
    return np.repeat(forward, 8, axis=0), np.repeat(forward, 4, axis=0)


def inverse_table():
    inverse = x_tables()[1].reshape(NX, 2 * K).T
    return np.repeat(inverse, 4, axis=0)


def mode_order():
    core, z, j2, l = np.meshgrid(np.arange(2), np.arange(4), np.arange(2), np.arange(K), indexing="ij")
    return (2 * (2 * z + core) + j2).reshape(-1), l.reshape(-1)


def cell_angles():
    j, l = mode_order()
    fj, fl = signed(j), signed(l)
    y = np.mod(fj[:, None] * np.arange(YL)[None, :], NY) / NY
    z = np.mod(fl[:, None] * np.arange(ZL)[None, :], NZ) / NZ
    turns = y[:, :, None] + z[:, None, :]
    return 2.0 * math.pi * turns.reshape(K * K, CELLS)


def mode_table():
    angles = cell_angles().T
    return np_bf16(np.concatenate([np.cos(angles), np.sin(angles)], 1))


def offset_phase(wide, narrow):
    lane = lax.broadcasted_iota(jnp.int32, (8, 256), 1)
    l = lane % 16
    j = 2 * (2 * ((lane // 32) % 4) + lane // 128) + (lane // 16) % 2
    fj = jnp.where(j < K // 2, j, j - K)
    fl = jnp.where(l < K // 2, l, l - K)
    step = (fj * wide + 2 * fl * narrow) & 15
    cos_v = jnp.zeros((8, 256), F32)
    sin_v = jnp.zeros((8, 256), F32)
    for k in range(16):
        c, s = math.cos(math.pi * k / 8), math.sin(math.pi * k / 8)
        cos_v = jnp.where(step == k, F32(c), cos_v)
        sin_v = jnp.where(step == k, F32(s), sin_v)
    return cos_v, sin_v


def row_of(pair, c):
    if c < 8:
        return pair * 8 + c
    if c < 16:
        return 16 + pair * 8 + c - 8
    return 32 + pair * 4 + c - 16


def block_turn(tiles):
    shape = tiles[0].shape
    block = lax.broadcasted_iota(jnp.int32, shape, len(shape) - 1) // 32
    out = []
    for r in range(4):
        v = tiles[r]
        for b in range(4):
            if b != r:
                v = jnp.where(block == b, pltpu.roll(tiles[b], (32 * (b - r)) % 128, len(shape) - 1), v)
        out.append(v)
    return out


def spectra_kernel(
    plume, w_hbm, t8_hbm, t4_hbm, e_ref, lw_hbm, bias_hbm, xi_hbm,
    m_ref, x_buf, e_buf, kron, rhs,
    w_ref, t8_ref, t4_ref, lw_ref, bias_ref, xi_ref, tab8, tab4, a_buf, sib_send, sib_recv, mine, s_send, s_recv, q_buf, wt_buf, m_send, m_recv,
    g_buf, phase,
    in_sem, w_sem, e_sem, c_ss, c_rs, s_ss, s_rs, m_ss, m_rs, g_ss, g_rs,
):
    wide, narrow = lax.axis_index("wide"), lax.axis_index("narrow")
    y, x = lax.div(wide, 4), lax.rem(wide, 4)
    z, core = lax.div(narrow, 2), lax.rem(narrow, 2)
    sibling = (wide, narrow + 1 - 2 * core)
    e_copy = pltpu.make_async_copy(e_ref, e_buf, e_sem)
    small = [pltpu.make_async_copy(src, dst, w_sem.at[i]) for i, (src, dst) in enumerate(
        ((t8_hbm, t8_ref), (t4_hbm, t4_ref), (w_hbm, w_ref), (lw_hbm, lw_ref), (bias_hbm, bias_ref),
         (xi_hbm, xi_ref)))]
    for copy in small[:2]:
        copy.start()
    loads = []
    for g, (c0, nc, _) in enumerate(GROUPS):
        copy = pltpu.make_async_copy(plume.at[pl.ds(c0, nc)], x_buf.at[pl.ds(c0, nc)], in_sem.at[g])
        copy.start()
        loads.append(copy)
        if g == 0:
            e_copy.start()
    for copy in small[2:]:
        copy.start()

    rows_of_chips = [4 * lax.rem(y + d, 4) for d in range(4)]
    places = [lax.rem(x + d, 4) for d in range(4)]
    wides = [[r + p for p in places] for r in rows_of_chips]
    layers = [lax.rem(z + d, 4) for d in range(4)]
    narrows = [2 * v + core for v in layers]
    far = (0, 1, 2, 1)
    others = sorted(
        [(16 * dz + 4 * dy + dx, dz, dy, dx) for dz in range(4) for dy in range(4) for dx in range(4)][1:],
        key=lambda v: (-(far[v[1]] + far[v[2]] + far[v[3]]), (v[0] * 37) % 64))

    barrier = pltpu.get_barrier_semaphore()
    pl.semaphore_signal(barrier, inc=1, device_id=sibling, device_id_type=MESH)

    for _, dz, dy, dx in others:
        pl.semaphore_signal(barrier, inc=1, device_id=(wides[dy][dx], narrows[dz]), device_id_type=MESH)

    for copy in small[:2]:
        copy.wait()
    r8 = lax.broadcasted_iota(jnp.int32, (256, NX), 0) % 8
    r4 = lax.broadcasted_iota(jnp.int32, (128, NX), 0) % 4
    for c in range(8):
        tab8[:, pl.ds(NX * c, NX)] = jnp.where(r8 == c, t8_ref[...], jnp.zeros((), BF16))
    for c in range(4):
        tab4[:, pl.ds(NX * c, NX)] = jnp.where(r4 == c, t4_ref[...], jnp.zeros((), BF16))
    cos_v, sin_v = offset_phase(wide, narrow)
    for h in range(2):
        phase[0, h] = cos_v[:, 128 * h:128 * h + 128]
        phase[1, h] = sin_v[:, 128 * h:128 * h + 128]
    scale = F32(1.0 / math.sqrt(NX * NY * NZ))
    pc, ps = cos_v * scale, sin_v * scale

    def c_copy(g):
        c0, nc, row0 = GROUPS[g]
        rows = pl.ds(row0, 32 * nc)
        return pltpu.make_async_remote_copy(
            src_ref=sib_send.at[1 - core, rows], dst_ref=sib_recv.at[rows],
            send_sem=c_ss.at[g], recv_sem=c_rs.at[g], device_id=sibling, device_id_type=MESH)

    for g, (c0, nc, row0) in enumerate(GROUPS):
        loads[g].wait()
        table = tab8 if nc == 8 else tab4
        width = 32 * nc
        for r in range(4):
            rows = jnp.concatenate(
                [x_buf[c, pl.ds(8 * r, 8)].reshape(256, NX) for c in range(c0, c0 + nc)], axis=1)
            a_buf[pl.ds(0, width), pl.ds(256 * r, 256)] = lax.dot_general(
                table[...], rows, CONTRACT_LANES, preferred_element_type=F32).astype(BF16)
        if g == 0:
            e_copy.wait()
        turned = jnp.dot(a_buf[pl.ds(0, width), :], e_buf[...], preferred_element_type=F32)
        g_cos = turned[:, :256].reshape(width // 8, 8, 256)
        g_sin = turned[:, 256:].reshape(width // 8, 8, 256)
        rc = pc * g_cos - ps * g_sin
        rs = ps * g_cos + pc * g_sin
        if nc == 8:
            rc, rs = rc.reshape(K, 2, 8, 256), rs.reshape(K, 2, 8, 256)
            s = jnp.stack([rc[:, 0] + rs[:, 1], rc[:, 1] - rs[:, 0]], axis=1)
        else:
            first = lax.broadcasted_iota(jnp.int32, (K, 8, 256), 1) < 4
            turn = pltpu.roll(rs, 4, 1)
            s = rc + jnp.where(first, turn, -turn)
        s = s.reshape(width, 256)
        sib_send[0, pl.ds(row0, width), :] = s[:, :128].astype(BF16)
        sib_send[1, pl.ds(row0, width), :] = s[:, 128:].astype(BF16)
        mine[pl.ds(row0, width), :] = jnp.where(core == 0, s[:, :128], s[:, 128:])
        if g == 0:
            pl.semaphore_wait(barrier, 64)
        c_copy(g).start()

    for g in range(len(GROUPS)):
        c_copy(g).wait_recv()

    def both(g, size):
        _, nc, row0 = GROUPS[g]
        rows = pl.ds(row0, 32 * nc)
        return (mine[rows, :] + sib_recv[rows, :].astype(F32)).reshape(size)

    g0, g1, g2 = both(0, (K, 2, 8, 128)), both(1, (K, 2, 8, 128)), both(2, (K, 8, 128))
    dense = block_turn([g0[:, 0], g0[:, 1], g1[:, 0], g1[:, 1]])
    for r in range(4):
        rest = g2 if r == 0 else pltpu.roll(g2, 128 - 32 * r, 2)
        s_send[r] = jnp.concatenate([dense[r], rest], axis=1).astype(BF16)

    for slot, dz, dy, dx in others:
        pltpu.make_async_remote_copy(
            src_ref=s_send.at[layers[dz], wides[dy][dx]], dst_ref=s_recv.at[slot],
            send_sem=s_ss, recv_sem=s_rs.at[dz],
            device_id=(wides[dy][dx], narrows[dz]), device_id_type=MESH).start()

    def arrived(buf, sems, part):
        ref = buf.at[pl.ds(max(1, 16 * part), 16 if part else 15)]
        pltpu.make_async_copy(ref, ref, sems.at[part]).wait()

    for copy in small[2:]:
        copy.wait()
    for k in range(7):
        width = min(128, 2 * C * C - 128 * k)
        wt_buf[pl.ds(128 * k, width), :] = w_ref[:, pl.ds(128 * k, width)].T
    spread = jnp.where(
        lax.broadcasted_iota(jnp.int32, (320, C), 0) // 16 == lax.broadcasted_iota(jnp.int32, (320, C), 1),
        F32(1.0), F32(0.0)).astype(BF16)
    rows20 = jnp.dot(spread, lw_ref[...], preferred_element_type=F32).astype(BF16)
    across = jnp.where(
        lax.broadcasted_iota(jnp.int32, (C, 384), 1) // 16 == lax.broadcasted_iota(jnp.int32, (C, 384), 0),
        F32(1.0), F32(0.0)).astype(BF16)
    full = jnp.dot(rows20, across, preferred_element_type=F32)
    row = lax.broadcasted_iota(jnp.int32, (320, 384), 0)
    col = lax.broadcasted_iota(jnp.int32, (320, 384), 1)
    full = jnp.where((row % 16) == (col % 16), full, F32(0.0))
    own = (lax.broadcasted_iota(jnp.int32, (320, C), 0) // 16 == lax.broadcasted_iota(jnp.int32, (320, C), 1))
    bias = jnp.sum(jnp.where(own, bias_ref[...], F32(0.0)), axis=1, keepdims=True)
    b1 = bias.astype(BF16).astype(F32)
    b2 = (bias - b1).astype(BF16).astype(F32)
    b3 = bias - b1 - b2
    full = jnp.where(col == 320, b1, full)
    full = jnp.where(col == 321, b2, full)
    full = jnp.where(col == 322, b3, full)
    kron[...] = full.astype(BF16)
    for s in range(2):
        rhs[s, pl.ds(0, 128), :] = xi_ref[...]
        rhs[s, pl.ds(192, 64), :] = jnp.where(
            lax.broadcasted_iota(jnp.int32, (64, NX), 0) < 16, F32(1.0), F32(0.0)).astype(BF16)
    total = s_send[z, wide].astype(F32)
    for part in (0, 1, 3, 2):
        first = max(1, 16 * part)
        arrived(s_recv, s_rs, part)
        total = total + jnp.sum(s_recv[pl.ds(first, 16 * part + 16 - first)].astype(F32), axis=0)
    for t in range(4):
        v = total[0:8] if t == 0 else pltpu.roll(total[0:8], 128 - 32 * t, 1)
        q_buf[pl.ds(8 * t, 8), :] = v[:, :32]
    q_buf[pl.ds(32, 8), :] = total[8:16, :32]

    out_re = jnp.zeros((C, 32), F32)
    out_im = jnp.zeros((C, 32), F32)
    for c in range(C):
        s_re = q_buf[pl.ds(row_of(0, c), 1), :]
        s_im = q_buf[pl.ds(row_of(1, c), 1), :]
        w_re = wt_buf[pl.ds(C * c, C), :]
        w_im = wt_buf[pl.ds(C * C + C * c, C), :]
        out_re = out_re + (w_re * s_re - w_im * s_im)
        out_im = out_im + (w_re * s_im + w_im * s_re)
    tiles = [jnp.concatenate([out_re[4 * j:4 * j + 4], out_im[4 * j:4 * j + 4]], axis=0) for j in range(5)]
    m_send[...] = jnp.concatenate(
        [jnp.concatenate(tiles[:4], axis=1),
         jnp.concatenate([tiles[4], jnp.zeros((8, 96), F32)], axis=1)], axis=0).astype(BF16)

    for slot, dz, dy, dx in others:
        pltpu.make_async_remote_copy(
            src_ref=m_send, dst_ref=m_recv.at[z, wide], send_sem=m_ss, recv_sem=m_rs,
            device_id=(wides[dy][dx], narrows[dz]), device_id_type=MESH).start()
    m_recv[z, wide] = m_send[...]

    def all_but_one(sem):
        ref = s_recv.at[pl.ds(1, 63)]
        pltpu.make_async_copy(ref, ref, sem).wait()

    all_but_one(m_rs)
    got = [m_recv[r].astype(F32) for r in range(4)]
    dense = block_turn([v[:, :8] for v in got])
    block = lax.broadcasted_iota(jnp.int32, (K, 8, 128), 2) // 32
    last = got[0][:, 8:]
    for r in range(1, 4):
        last = jnp.where(block == r, pltpu.roll(got[r][:, 8:], 32 * r, 2), last)
    def g_copy(j):
        rows = pl.ds(128 * j, 128)
        return pltpu.make_async_remote_copy(
            src_ref=g_buf.at[core, rows], dst_ref=g_buf.at[core, rows], send_sem=g_ss.at[j], recv_sem=g_rs.at[j],
            device_id=sibling, device_id_type=MESH)

    for j, v in enumerate(dense + [last]):
        g_buf[core, pl.ds(128 * j, 128), :] = v.reshape(128, 128).astype(BF16)
        g_copy(j).start()

    def place(half):
        v = g_buf[half].astype(F32).reshape(80, 8, 128)
        turn = pltpu.roll(v, 4, 1)
        sw = jnp.where(lax.broadcasted_iota(jnp.int32, (80, 8, 128), 1) < 4, -turn, turn)
        c_half, s_half = phase[0, half], phase[1, half]
        at = pl.multiple_of(128 * half, 128)
        m_ref[:, pl.ds(at, 128)] = (c_half * v + s_half * sw).reshape(LANES, 128).astype(BF16)
        m_ref[:, pl.ds(256 + at, 128)] = (c_half * sw - s_half * v).reshape(LANES, 128).astype(BF16)

    place(core)

    all_but_one(s_ss)
    all_but_one(m_ss)
    for g in range(len(GROUPS)):
        c_copy(g).wait_send()
    for j in range(5):
        g_copy(j).wait_recv()
    place(1 - core)
    for j in range(5):
        g_copy(j).wait_send()


def spectra(plume, weight, t8, t4, e, lw, bias, xi):
    vmem = pl.BlockSpec(memory_space=pltpu.VMEM)
    anywhere = pl.BlockSpec(memory_space=pl.ANY)
    dma = pltpu.SemaphoreType.DMA
    return pl.pallas_call(
        spectra_kernel,
        out_shape=(
            pltpu.VMEM((LANES, 2 * K * K), BF16),
            pltpu.VMEM((C, YL, ZL, NX), BF16),
            pltpu.VMEM((CELLS, 512), BF16),
            pltpu.VMEM((320, 384), BF16),
            pltpu.VMEM((2, 256, NX), BF16),
        ),
        in_specs=[anywhere] * 8,
        out_specs=(vmem,) * 5,
        scratch_shapes=[
            pltpu.VMEM((32, 2 * C * C), F32),
            pltpu.VMEM((256, NX), BF16),
            pltpu.VMEM((128, NX), BF16),
            pltpu.VMEM((C, C), BF16),
            pltpu.VMEM((1, C), F32),
            pltpu.VMEM((128, NX), BF16),
            pltpu.VMEM((256, 8 * NX), BF16),
            pltpu.VMEM((128, 4 * NX), BF16),
            pltpu.VMEM((256, CELLS), BF16),
            pltpu.VMEM((2, LANES, 128), BF16),
            pltpu.VMEM((LANES, 128), BF16),
            pltpu.VMEM((LANES, 128), F32),
            pltpu.VMEM((4, 16, 16, 128), BF16),
            pltpu.VMEM((64, 16, 128), BF16),
            pltpu.VMEM((40, 32), F32),
            pltpu.VMEM((2 * C * C, 32), F32),
            pltpu.VMEM((16, 128), BF16),
            pltpu.VMEM((4, 16, 16, 128), BF16),
            pltpu.VMEM((2, LANES, 128), BF16),
            pltpu.VMEM((2, 2, 8, 128), F32),
            dma((3,)), dma((6,)), dma,
            dma((3,)), dma((3,)),
            dma, dma((4,)),
            dma, dma,
            dma((5,)), dma((5,)),
        ],
        compiler_params=pltpu.CompilerParams(
            collective_id=0, has_side_effects=True, vmem_limit_bytes=51 * 2**20),
        name="spectra",
    )(plume, weight, t8, t4, e, lw, bias, xi)


CHUNKS = 2
STORED = 2


def output_kernel(m_ref, x_buf, e_ref, kron, rhs, out, o_buf, b_buf, out_sem):
    yt = YL // CHUNKS

    def store(i):
        rows = pl.ds(i * STORED, STORED)
        return pltpu.make_async_copy(o_buf.at[:, rows], out.at[:, rows], out_sem.at[i])

    lane = lax.broadcasted_iota(jnp.int32, (16, 128), 1) % 4
    masks = [lane == k for k in range(4)]

    def chunk(i, _):
        cells = yt * ZL
        b_buf[...] = lax.dot_general(
            e_ref[pl.ds(pl.multiple_of(i * cells, cells), cells), :], m_ref[...], CONTRACT_LANES,
            preferred_element_type=F32).astype(BF16)
        for q in range(cells // 16):
            y, z, s = i * yt + q // 2, (q % 2) * 16, q % 2
            xs = x_buf[:, y, pl.ds(z, 16), :].reshape(320, NX)
            parts = []
            for o in range(C):
                v = b_buf[pl.ds(16 * q, 16), pl.ds(128 * (o // 4), 128)]
                parts.append(jnp.where(masks[o % 4], v, jnp.zeros_like(v)))
            left = jnp.concatenate([jnp.concatenate(parts, 0), kron[:, pl.ds(256, 128)]], 1)
            left = jnp.concatenate([kron[:, pl.ds(0, 256)], left], 1)
            right = jnp.concatenate(
                [xs[:256], rhs[0, pl.ds(0, 128), :], xs[256:], rhs[0, pl.ds(192, 64), :]], 0)
            for h in range(2):
                acc = jnp.dot(left[160 * h:160 * h + 160], right, preferred_element_type=F32)
                half = 0.5 * acc
                y_out = half + half * lax.erf(acc * F32(math.sqrt(0.5)))
                o_buf[pl.ds(10 * h, 10), y, pl.ds(z, 16), :] = y_out.astype(BF16).reshape(10, 16, NX)
            if q % (2 * STORED) == 2 * STORED - 1:
                store(i * (yt // STORED) + q // (2 * STORED)).start()
        return 0

    lax.fori_loop(0, CHUNKS, chunk, 0)
    for i in range(YL // STORED):
        store(i).wait()


def output(m, x, e, kron, rhs):
    vmem = pl.BlockSpec(memory_space=pltpu.VMEM)
    return pl.pallas_call(
        output_kernel,
        out_shape=jax.ShapeDtypeStruct((C, YL, ZL, NX), BF16),
        in_specs=[vmem] * 5,
        out_specs=pl.BlockSpec(memory_space=pltpu.HBM),
        scratch_shapes=[
            pltpu.VMEM((C, YL, ZL, NX), BF16),
            pltpu.VMEM((CELLS // CHUNKS, LANES), BF16),
            pltpu.SemaphoreType.DMA((YL // STORED,)),
        ],
        compiler_params=pltpu.CompilerParams(vmem_limit_bytes=16 * 2**20),
        name="output",
    )(m, x, e, kron, rhs)


def on_device(plume, weight, linear_weight, channel_bias):
    t8, t4 = forward_table()
    return output(*spectra(
        plume, weight.reshape(32, 2 * C * C), jnp.asarray(t8), jnp.asarray(t4), jnp.asarray(mode_table()),
        linear_weight, channel_bias.reshape(1, C), jnp.asarray(inverse_table())))


def solution(mesh):
    return jax.shard_map(
        on_device, mesh=mesh,
        in_specs=(P(None, "wide", "narrow", None), P("wide", "narrow", None, None), P(), P()),
        out_specs=P(None, "wide", "narrow", None), check_vma=False)
```

```python
import math

import jax
import jax.numpy as jnp
import ml_dtypes
import numpy as np
from jax import lax
from jax.experimental import pallas as pl
from jax.experimental.pallas import tpu as pltpu
from jax.sharding import PartitionSpec as P

MESH = pl.DeviceIdType.MESH
C, NX, NY, NZ, K = 20, 256, 512, 256, 16
YL, ZL = 32, 32
CELLS = YL * ZL
LANES = 2 * K * C
BF16, F32 = jnp.bfloat16, jnp.float32
GROUPS = ((0, 8, 0), (8, 8, 256), (16, 4, 512))
CONTRACT_LANES = (((1,), (1,)), ((), ()))


def np_bf16(a):
    return np.asarray(a, np.float32).astype(ml_dtypes.bfloat16)


def signed(m):
    return np.where(m < K // 2, m, m - K)


def x_tables():
    places, orders = np.arange(NX), np.arange(K)
    angles = np.mod(places[:, None] * orders[None, :], NX).astype(np.float32) * np.float32(2.0 * math.pi / NX)
    cos_tab, sin_tab = np.cos(angles), np.sin(angles)
    doubled = np.where(orders == 0, 1.0, 2.0).astype(np.float32)
    forward = np_bf16(np.stack([cos_tab, -sin_tab], -1))
    inverse = np_bf16(np.stack([cos_tab * doubled, -sin_tab * doubled], -1))
    return forward, inverse


def forward_table():
    forward = x_tables()[0].reshape(NX, 2 * K).T
    return np.repeat(forward, 8, axis=0), np.repeat(forward, 4, axis=0)


def inverse_table():
    inverse = x_tables()[1].reshape(NX, 2 * K).T
    return np.repeat(inverse, 4, axis=0)


def mode_order():
    core, z, j2, l = np.meshgrid(np.arange(2), np.arange(4), np.arange(2), np.arange(K), indexing="ij")
    return (2 * (2 * z + core) + j2).reshape(-1), l.reshape(-1)


def cell_angles():
    j, l = mode_order()
    fj, fl = signed(j), signed(l)
    y = np.mod(fj[:, None] * np.arange(YL)[None, :], NY) / NY
    z = np.mod(fl[:, None] * np.arange(ZL)[None, :], NZ) / NZ
    turns = y[:, :, None] + z[:, None, :]
    return 2.0 * math.pi * turns.reshape(K * K, CELLS)


def mode_table():
    angles = cell_angles().T
    return np_bf16(np.concatenate([np.cos(angles), np.sin(angles)], 1))


def offset_phase(wide, narrow):
    lane = lax.broadcasted_iota(jnp.int32, (8, 256), 1)
    l = lane % 16
    j = 2 * (2 * ((lane // 32) % 4) + lane // 128) + (lane // 16) % 2
    fj = jnp.where(j < K // 2, j, j - K)
    fl = jnp.where(l < K // 2, l, l - K)
    step = (fj * wide + 2 * fl * narrow) & 15
    cos_v = jnp.zeros((8, 256), F32)
    sin_v = jnp.zeros((8, 256), F32)
    for k in range(16):
        c, s = math.cos(math.pi * k / 8), math.sin(math.pi * k / 8)
        cos_v = jnp.where(step == k, F32(c), cos_v)
        sin_v = jnp.where(step == k, F32(s), sin_v)
    return cos_v, sin_v


def row_of(pair, c):
    if c < 8:
        return pair * 8 + c
    if c < 16:
        return 16 + pair * 8 + c - 8
    return 32 + pair * 4 + c - 16


def block_turn(tiles):
    shape = tiles[0].shape
    block = lax.broadcasted_iota(jnp.int32, shape, len(shape) - 1) // 32
    out = []
    for r in range(4):
        v = tiles[r]
        for b in range(4):
            if b != r:
                v = jnp.where(block == b, pltpu.roll(tiles[b], (32 * (b - r)) % 128, len(shape) - 1), v)
        out.append(v)
    return out


def spectra_kernel(
    plume, w_hbm, t8_hbm, t4_hbm, e_ref, lw_hbm, bias_hbm, xi_hbm,
    m_ref, x_buf, e_buf, kron, rhs,
    w_ref, t8_ref, t4_ref, lw_ref, bias_ref, xi_ref, tab8, tab4, a_buf, sib_send, sib_recv, mine, s_send, s_recv, q_buf, wt_buf, m_send, m_recv,
    g_buf, phase,
    in_sem, w_sem, e_sem, c_ss, c_rs, s_ss, s_rs, m_ss, m_rs, g_ss, g_rs,
):
    wide, narrow = lax.axis_index("wide"), lax.axis_index("narrow")
    y, x = lax.div(wide, 4), lax.rem(wide, 4)
    z, core = lax.div(narrow, 2), lax.rem(narrow, 2)
    sibling = (wide, narrow + 1 - 2 * core)
    e_copy = pltpu.make_async_copy(e_ref, e_buf, e_sem)
    small = [pltpu.make_async_copy(src, dst, w_sem.at[i]) for i, (src, dst) in enumerate(
        ((t8_hbm, t8_ref), (t4_hbm, t4_ref), (w_hbm, w_ref), (lw_hbm, lw_ref), (bias_hbm, bias_ref),
         (xi_hbm, xi_ref)))]
    for copy in small[:2]:
        copy.start()
    loads = []
    for g, (c0, nc, _) in enumerate(GROUPS):
        copy = pltpu.make_async_copy(plume.at[pl.ds(c0, nc)], x_buf.at[pl.ds(c0, nc)], in_sem.at[g])
        copy.start()
        loads.append(copy)
        if g == 0:
            e_copy.start()
    for copy in small[2:]:
        copy.start()

    rows_of_chips = [4 * lax.rem(y + d, 4) for d in range(4)]
    places = [lax.rem(x + d, 4) for d in range(4)]
    wides = [[r + p for p in places] for r in rows_of_chips]
    layers = [lax.rem(z + d, 4) for d in range(4)]
    narrows = [2 * v + core for v in layers]
    far = (0, 1, 2, 1)
    others = sorted(
        [(16 * dz + 4 * dy + dx, dz, dy, dx) for dz in range(4) for dy in range(4) for dx in range(4)][1:],
        key=lambda v: (-(far[v[1]] + far[v[2]] + far[v[3]]), (v[0] * 21) % 64))

    barrier = pltpu.get_barrier_semaphore()
    pl.semaphore_signal(barrier, inc=1, device_id=sibling, device_id_type=MESH)

    for _, dz, dy, dx in others:
        pl.semaphore_signal(barrier, inc=1, device_id=(wides[dy][dx], narrows[dz]), device_id_type=MESH)

    for copy in small[:2]:
        copy.wait()
    r8 = lax.broadcasted_iota(jnp.int32, (256, NX), 0) % 8
    r4 = lax.broadcasted_iota(jnp.int32, (128, NX), 0) % 4
    for c in range(8):
        tab8[:, pl.ds(NX * c, NX)] = jnp.where(r8 == c, t8_ref[...], jnp.zeros((), BF16))
    for c in range(4):
        tab4[:, pl.ds(NX * c, NX)] = jnp.where(r4 == c, t4_ref[...], jnp.zeros((), BF16))
    cos_v, sin_v = offset_phase(wide, narrow)
    for h in range(2):
        phase[0, h] = cos_v[:, 128 * h:128 * h + 128]
        phase[1, h] = sin_v[:, 128 * h:128 * h + 128]
    scale = F32(1.0 / math.sqrt(NX * NY * NZ))
    pc, ps = cos_v * scale, sin_v * scale

    def c_copy(g):
        c0, nc, row0 = GROUPS[g]
        rows = pl.ds(row0, 32 * nc)
        return pltpu.make_async_remote_copy(
            src_ref=sib_send.at[1 - core, rows], dst_ref=sib_recv.at[rows],
            send_sem=c_ss.at[g], recv_sem=c_rs.at[g], device_id=sibling, device_id_type=MESH)

    for g, (c0, nc, row0) in enumerate(GROUPS):
        loads[g].wait()
        table = tab8 if nc == 8 else tab4
        width = 32 * nc
        for r in range(4):
            rows = jnp.concatenate(
                [x_buf[c, pl.ds(8 * r, 8)].reshape(256, NX) for c in range(c0, c0 + nc)], axis=1)
            a_buf[pl.ds(0, width), pl.ds(256 * r, 256)] = lax.dot_general(
                table[...], rows, CONTRACT_LANES, preferred_element_type=F32).astype(BF16)
        if g == 0:
            e_copy.wait()
        turned = jnp.dot(a_buf[pl.ds(0, width), :], e_buf[...], preferred_element_type=F32)
        g_cos = turned[:, :256].reshape(width // 8, 8, 256)
        g_sin = turned[:, 256:].reshape(width // 8, 8, 256)
        rc = pc * g_cos - ps * g_sin
        rs = ps * g_cos + pc * g_sin
        if nc == 8:
            rc, rs = rc.reshape(K, 2, 8, 256), rs.reshape(K, 2, 8, 256)
            s = jnp.stack([rc[:, 0] + rs[:, 1], rc[:, 1] - rs[:, 0]], axis=1)
        else:
            first = lax.broadcasted_iota(jnp.int32, (K, 8, 256), 1) < 4
            turn = pltpu.roll(rs, 4, 1)
            s = rc + jnp.where(first, turn, -turn)
        s = s.reshape(width, 256)
        sib_send[0, pl.ds(row0, width), :] = s[:, :128].astype(BF16)
        sib_send[1, pl.ds(row0, width), :] = s[:, 128:].astype(BF16)
        mine[pl.ds(row0, width), :] = jnp.where(core == 0, s[:, :128], s[:, 128:])
        if g == 0:
            pl.semaphore_wait(barrier, 64)
        c_copy(g).start()

    for g in range(len(GROUPS)):
        c_copy(g).wait_recv()

    def both(g, size):
        _, nc, row0 = GROUPS[g]
        rows = pl.ds(row0, 32 * nc)
        return (mine[rows, :] + sib_recv[rows, :].astype(F32)).reshape(size)

    g0, g1, g2 = both(0, (K, 2, 8, 128)), both(1, (K, 2, 8, 128)), both(2, (K, 8, 128))
    dense = block_turn([g0[:, 0], g0[:, 1], g1[:, 0], g1[:, 1]])
    for r in range(4):
        rest = g2 if r == 0 else pltpu.roll(g2, 128 - 32 * r, 2)
        s_send[r] = jnp.concatenate([dense[r], rest], axis=1).astype(BF16)

    for slot, dz, dy, dx in others:
        pltpu.make_async_remote_copy(
            src_ref=s_send.at[layers[dz], wides[dy][dx]], dst_ref=s_recv.at[slot],
            send_sem=s_ss, recv_sem=s_rs.at[dz],
            device_id=(wides[dy][dx], narrows[dz]), device_id_type=MESH).start()

    def arrived(buf, sems, part):
        ref = buf.at[pl.ds(max(1, 16 * part), 16 if part else 15)]
        pltpu.make_async_copy(ref, ref, sems.at[part]).wait()

    for copy in small[2:]:
        copy.wait()
    for k in range(7):
        width = min(128, 2 * C * C - 128 * k)
        wt_buf[pl.ds(128 * k, width), :] = w_ref[:, pl.ds(128 * k, width)].T
    spread = jnp.where(
        lax.broadcasted_iota(jnp.int32, (320, C), 0) // 16 == lax.broadcasted_iota(jnp.int32, (320, C), 1),
        F32(1.0), F32(0.0)).astype(BF16)
    rows20 = jnp.dot(spread, lw_ref[...], preferred_element_type=F32).astype(BF16)
    across = jnp.where(
        lax.broadcasted_iota(jnp.int32, (C, 384), 1) // 16 == lax.broadcasted_iota(jnp.int32, (C, 384), 0),
        F32(1.0), F32(0.0)).astype(BF16)
    full = jnp.dot(rows20, across, preferred_element_type=F32)
    row = lax.broadcasted_iota(jnp.int32, (320, 384), 0)
    col = lax.broadcasted_iota(jnp.int32, (320, 384), 1)
    full = jnp.where((row % 16) == (col % 16), full, F32(0.0))
    own = (lax.broadcasted_iota(jnp.int32, (320, C), 0) // 16 == lax.broadcasted_iota(jnp.int32, (320, C), 1))
    bias = jnp.sum(jnp.where(own, bias_ref[...], F32(0.0)), axis=1, keepdims=True)
    b1 = bias.astype(BF16).astype(F32)
    b2 = (bias - b1).astype(BF16).astype(F32)
    b3 = bias - b1 - b2
    full = jnp.where(col == 320, b1, full)
    full = jnp.where(col == 321, b2, full)
    full = jnp.where(col == 322, b3, full)
    kron[...] = full.astype(BF16)
    for s in range(2):
        rhs[s, pl.ds(0, 128), :] = xi_ref[...]
        rhs[s, pl.ds(192, 64), :] = jnp.where(
            lax.broadcasted_iota(jnp.int32, (64, NX), 0) < 16, F32(1.0), F32(0.0)).astype(BF16)
    total = s_send[z, wide].astype(F32)
    for part in (0, 1, 3, 2):
        first = max(1, 16 * part)
        arrived(s_recv, s_rs, part)
        total = total + jnp.sum(s_recv[pl.ds(first, 16 * part + 16 - first)].astype(F32), axis=0)
    for t in range(4):
        v = total[0:8] if t == 0 else pltpu.roll(total[0:8], 128 - 32 * t, 1)
        q_buf[pl.ds(8 * t, 8), :] = v[:, :32]
    q_buf[pl.ds(32, 8), :] = total[8:16, :32]

    out_re = jnp.zeros((C, 32), F32)
    out_im = jnp.zeros((C, 32), F32)
    for c in range(C):
        s_re = q_buf[pl.ds(row_of(0, c), 1), :]
        s_im = q_buf[pl.ds(row_of(1, c), 1), :]
        w_re = wt_buf[pl.ds(C * c, C), :]
        w_im = wt_buf[pl.ds(C * C + C * c, C), :]
        out_re = out_re + (w_re * s_re - w_im * s_im)
        out_im = out_im + (w_re * s_im + w_im * s_re)
    tiles = [jnp.concatenate([out_re[4 * j:4 * j + 4], out_im[4 * j:4 * j + 4]], axis=0) for j in range(5)]
    m_send[...] = jnp.concatenate(
        [jnp.concatenate(tiles[:4], axis=1),
         jnp.concatenate([tiles[4], jnp.zeros((8, 96), F32)], axis=1)], axis=0).astype(BF16)

    for slot, dz, dy, dx in others:
        pltpu.make_async_remote_copy(
            src_ref=m_send, dst_ref=m_recv.at[z, wide], send_sem=m_ss, recv_sem=m_rs,
            device_id=(wides[dy][dx], narrows[dz]), device_id_type=MESH).start()
    m_recv[z, wide] = m_send[...]

    def all_but_one(sem):
        ref = s_recv.at[pl.ds(1, 63)]
        pltpu.make_async_copy(ref, ref, sem).wait()

    all_but_one(m_rs)
    got = [m_recv[r].astype(F32) for r in range(4)]
    dense = block_turn([v[:, :8] for v in got])
    block = lax.broadcasted_iota(jnp.int32, (K, 8, 128), 2) // 32
    last = got[0][:, 8:]
    for r in range(1, 4):
        last = jnp.where(block == r, pltpu.roll(got[r][:, 8:], 32 * r, 2), last)
    def g_copy(j):
        rows = pl.ds(128 * j, 128)
        return pltpu.make_async_remote_copy(
            src_ref=g_buf.at[core, rows], dst_ref=g_buf.at[core, rows], send_sem=g_ss.at[j], recv_sem=g_rs.at[j],
            device_id=sibling, device_id_type=MESH)

    for j, v in enumerate(dense + [last]):
        g_buf[core, pl.ds(128 * j, 128), :] = v.reshape(128, 128).astype(BF16)
        g_copy(j).start()

    def place(half):
        v = g_buf[half].astype(F32).reshape(80, 8, 128)
        turn = pltpu.roll(v, 4, 1)
        sw = jnp.where(lax.broadcasted_iota(jnp.int32, (80, 8, 128), 1) < 4, -turn, turn)
        c_half, s_half = phase[0, half], phase[1, half]
        at = pl.multiple_of(128 * half, 128)
        m_ref[:, pl.ds(at, 128)] = (c_half * v + s_half * sw).reshape(LANES, 128).astype(BF16)
        m_ref[:, pl.ds(256 + at, 128)] = (c_half * sw - s_half * v).reshape(LANES, 128).astype(BF16)

    place(core)

    all_but_one(s_ss)
    all_but_one(m_ss)
    for g in range(len(GROUPS)):
        c_copy(g).wait_send()
    for j in range(5):
        g_copy(j).wait_recv()
    place(1 - core)
    for j in range(5):
        g_copy(j).wait_send()


def spectra(plume, weight, t8, t4, e, lw, bias, xi):
    vmem = pl.BlockSpec(memory_space=pltpu.VMEM)
    anywhere = pl.BlockSpec(memory_space=pl.ANY)
    dma = pltpu.SemaphoreType.DMA
    return pl.pallas_call(
        spectra_kernel,
        out_shape=(
            pltpu.VMEM((LANES, 2 * K * K), BF16),
            pltpu.VMEM((C, YL, ZL, NX), BF16),
            pltpu.VMEM((CELLS, 512), BF16),
            pltpu.VMEM((320, 384), BF16),
            pltpu.VMEM((2, 256, NX), BF16),
        ),
        in_specs=[anywhere] * 8,
        out_specs=(vmem,) * 5,
        scratch_shapes=[
            pltpu.VMEM((32, 2 * C * C), F32),
            pltpu.VMEM((256, NX), BF16),
            pltpu.VMEM((128, NX), BF16),
            pltpu.VMEM((C, C), BF16),
            pltpu.VMEM((1, C), F32),
            pltpu.VMEM((128, NX), BF16),
            pltpu.VMEM((256, 8 * NX), BF16),
            pltpu.VMEM((128, 4 * NX), BF16),
            pltpu.VMEM((256, CELLS), BF16),
            pltpu.VMEM((2, LANES, 128), BF16),
            pltpu.VMEM((LANES, 128), BF16),
            pltpu.VMEM((LANES, 128), F32),
            pltpu.VMEM((4, 16, 16, 128), BF16),
            pltpu.VMEM((64, 16, 128), BF16),
            pltpu.VMEM((40, 32), F32),
            pltpu.VMEM((2 * C * C, 32), F32),
            pltpu.VMEM((16, 128), BF16),
            pltpu.VMEM((4, 16, 16, 128), BF16),
            pltpu.VMEM((2, LANES, 128), BF16),
            pltpu.VMEM((2, 2, 8, 128), F32),
            dma((3,)), dma((6,)), dma,
            dma((3,)), dma((3,)),
            dma, dma((4,)),
            dma, dma,
            dma((5,)), dma((5,)),
        ],
        compiler_params=pltpu.CompilerParams(
            collective_id=0, has_side_effects=True, vmem_limit_bytes=51 * 2**20),
        name="spectra",
    )(plume, weight, t8, t4, e, lw, bias, xi)


CHUNKS = 2
STORED = 1


def output_kernel(m_ref, x_buf, e_ref, kron, rhs, out, o_buf, b_buf, out_sem):
    yt = YL // CHUNKS

    def store(i):
        rows = pl.ds(i * STORED, STORED)
        return pltpu.make_async_copy(o_buf.at[:, rows], out.at[:, rows], out_sem.at[i])

    lane = lax.broadcasted_iota(jnp.int32, (16, 128), 1) % 4
    masks = [lane == k for k in range(4)]

    def chunk(i, _):
        cells = yt * ZL
        b_buf[...] = lax.dot_general(
            e_ref[pl.ds(pl.multiple_of(i * cells, cells), cells), :], m_ref[...], CONTRACT_LANES,
            preferred_element_type=F32).astype(BF16)
        for q in range(cells // 16):
            y, z, s = i * yt + q // 2, (q % 2) * 16, q % 2
            xs = x_buf[:, y, pl.ds(z, 16), :].reshape(320, NX)
            parts = []
            for o in range(C):
                v = b_buf[pl.ds(16 * q, 16), pl.ds(128 * (o // 4), 128)]
                parts.append(jnp.where(masks[o % 4], v, jnp.zeros_like(v)))
            left = jnp.concatenate([jnp.concatenate(parts, 0), kron[:, pl.ds(256, 128)]], 1)
            left = jnp.concatenate([kron[:, pl.ds(0, 256)], left], 1)
            right = jnp.concatenate(
                [xs[:256], rhs[0, pl.ds(0, 128), :], xs[256:], rhs[0, pl.ds(192, 64), :]], 0)
            for h in range(2):
                acc = jnp.dot(left[160 * h:160 * h + 160], right, preferred_element_type=F32)
                half = 0.5 * acc
                y_out = half + half * lax.erf(acc * F32(math.sqrt(0.5)))
                o_buf[pl.ds(10 * h, 10), y, pl.ds(z, 16), :] = y_out.astype(BF16).reshape(10, 16, NX)
            if q % (2 * STORED) == 2 * STORED - 1:
                store(i * (yt // STORED) + q // (2 * STORED)).start()
        return 0

    lax.fori_loop(0, CHUNKS, chunk, 0)
    for i in range(YL // STORED):
        store(i).wait()


def output(m, x, e, kron, rhs):
    vmem = pl.BlockSpec(memory_space=pltpu.VMEM)
    return pl.pallas_call(
        output_kernel,
        out_shape=jax.ShapeDtypeStruct((C, YL, ZL, NX), BF16),
        in_specs=[vmem] * 5,
        out_specs=pl.BlockSpec(memory_space=pltpu.HBM),
        scratch_shapes=[
            pltpu.VMEM((C, YL, ZL, NX), BF16),
            pltpu.VMEM((CELLS // CHUNKS, LANES), BF16),
            pltpu.SemaphoreType.DMA((YL // STORED,)),
        ],
        compiler_params=pltpu.CompilerParams(vmem_limit_bytes=16 * 2**20),
        name="output",
    )(m, x, e, kron, rhs)


def on_device(plume, weight, linear_weight, channel_bias):
    t8, t4 = forward_table()
    return output(*spectra(
        plume, weight.reshape(32, 2 * C * C), jnp.asarray(t8), jnp.asarray(t4), jnp.asarray(mode_table()),
        linear_weight, channel_bias.reshape(1, C), jnp.asarray(inverse_table())))


def solution(mesh):
    return jax.shard_map(
        on_device, mesh=mesh,
        in_specs=(P(None, "wide", "narrow", None), P("wide", "narrow", None, None), P(), P()),
        out_specs=P(None, "wide", "narrow", None), check_vma=False)
```
